512 devices in a mesh: ctx: 32 (over y, x, core), tp: 16 (over z).
Axes of the slice: x: 4, y: 4, z: 16, core: 2. Of those that a mesh axis runs over, the one named last changes fastest.
Arguments:
- queries: bfloat16 [8192, 4096], P('ctx', 'tp'), may hold values from -6 to 6
- keys: bfloat16 [8192, 2048], P('ctx', 'tp'), may hold values from -6 to 6
- values: bfloat16 [8192, 2048], P('ctx', 'tp'), may hold values from -6 to 6
- out_weight: bfloat16 [4096, 5120], P('tp'), may hold values from -0.09375 to 0.09375
- residual: bfloat16 [8192, 5120], P(('ctx', 'tp')), may hold values from -6 to 6
- norm_gain: float32 [5120], replicated, may hold values from 0.5 to 1.5
- lengths: int32 [32], replicated, may hold values from 1 to 4096, as said below
- owner_blocks: int32 [32, 2], replicated, may hold values from 0 to 63, as said below
Outputs:
- mixed: bfloat16 [8192, 5120], P(('ctx', 'tp'))
The draws below stay inside these ranges and needn't reach their ends.
Inputs may be any that keep to these rules, and one draw needn't show every extreme that they name: 32 positive lengths that sum to 8192; one is exactly 4096. `owner_blocks`: every block number 0 to 63 appears exactly once; block b lies on index b // 2 of ctx, and the 2 blocks of one row lie on 2 different indices of ctx.
All inputs are finite; a program needn't handle non-finite values.
Results may differ from the reference program's by a relative error of at most 0.019.
Values may be sent and summed in bfloat16 or wider, within the bound.
A program may use at most 64 MiB of HBM per device.

```python
import math
import jax
import jax.numpy as jnp
from jax import lax

D = 5120
HD = 128
HEADS_DEV = 2
BLOCK = 128
BLK_DEV = 2
HEADS = 32
KV_HEADS = 16
TOK_DEV = 256
SEQ = 8192
DOCS = 32
MAXDOC = 4096
N_CTX = 32
N_TP = 16


def doc_lengths(key):
    first_key, second_key = jax.random.split(jax.random.fold_in(key, 101))
    longest = jax.random.randint(first_key, (), 0, DOCS)
    shares = jax.random.randint(second_key, (DOCS,), 1, 100)
    slots = jnp.arange(DOCS)
    shares = jnp.where(slots == longest, 0, shares)
    spare = SEQ - MAXDOC - (DOCS - 1)
    portion = spare * shares // jnp.sum(shares)
    sizes = jnp.where(slots == longest, MAXDOC, 1 + portion)
    missing = SEQ - jnp.sum(sizes)
    last_small = jnp.where(longest == DOCS - 1, DOCS - 2, DOCS - 1)
    sizes = sizes + jnp.where(slots == last_small, missing, 0)
    return sizes.astype(jnp.int32)


def draw_lengths(key, part):
    return doc_lengths(key)


def draw_owner_blocks(key, part):
    sizes = doc_lengths(key)
    ends = jnp.cumsum(sizes)
    starts = ends - sizes
    positions = jnp.arange(SEQ, dtype=jnp.int32)
    doc = jnp.sum((positions[:, None] >= ends[None, :]).astype(jnp.int32), axis=1)
    offset = positions - starts[doc] + 1
    source_cost = jnp.sum(offset.reshape(N_CTX, TOK_DEV), axis=1)
    score = source_cost * N_CTX + jnp.arange(N_CTX, dtype=jnp.int32)
    ranked = jnp.argsort(-score).astype(jnp.int32)
    sigma = jnp.zeros((N_CTX,), jnp.int32).at[ranked].set(jnp.arange(N_CTX, dtype=jnp.int32))
    slots = jnp.arange(BLK_DEV, dtype=jnp.int32)
    stride = N_CTX // BLK_DEV
    owner = (sigma[:, None] + slots[None, :] * stride) % N_CTX
    blocks = jnp.arange(N_CTX, dtype=jnp.int32)[:, None] * BLK_DEV + slots[None, :]
    slot_grid = jnp.broadcast_to(slots[None, :], (N_CTX, BLK_DEV))
    table = jnp.zeros((N_CTX, BLK_DEV), jnp.int32)
    return table.at[owner.reshape(-1), slot_grid.reshape(-1)].set(blocks.reshape(-1))


def draw_queries(key, part):
    key = jax.random.fold_in(key, 5)
    base_draw = jnp.clip(jax.random.normal(key, (SEQ, KV_HEADS, 2, HD)), -6.0, 6.0)
    return base_draw.reshape(SEQ, HEADS * HD).astype(jnp.bfloat16)


def draw_keys(key, part):
    key = jax.random.fold_in(key, 7)
    base_draw = jnp.clip(jax.random.normal(key, (SEQ, KV_HEADS, HD)), -6.0, 6.0)
    return base_draw.reshape(SEQ, KV_HEADS * HD).astype(jnp.bfloat16)


def steps_of(key, dims, cuts, smallest, largest):
    loudness = 1.0
    for dim, shards_of in cuts:
        draws = jax.random.uniform(jax.random.fold_in(jax.random.fold_in(key, 6), dim), (shards_of,), jnp.float32, smallest / len(cuts), largest / len(cuts))
        loudness = loudness * jnp.repeat(jnp.exp(draws), dims[dim] // shards_of).reshape((-1,) + (1,) * (len(dims) - 1 - dim))
    return loudness


def noise(own_key, shape, deviation, bound, cuts=(), kind=jnp.bfloat16):
    drawn = deviation * jax.random.normal(own_key, shape, jnp.float32)
    if cuts:
        drawn = drawn * steps_of(own_key, shape, cuts, -0.22, 0.18)
    return jnp.clip(drawn, -bound, bound).astype(kind)


def setup_inputs(seed: int = 0) -> dict:
    key_of = jax.random.split(jax.random.key(seed), 9)
    queries = draw_queries(jax.random.fold_in(key_of[8], 71), 0)
    keys = draw_keys(jax.random.fold_in(key_of[8], 71), 0)
    values = noise(key_of[2], (SEQ, KV_HEADS * HD), 1.0, 6.0, ((0, 32), (1, 16)))
    out_weight = noise(key_of[3], (HEADS * HD, D), (HEADS * HD) ** -0.5, 0.09375, ((0, 16),))
    residual = noise(key_of[4], (SEQ, D), 1.0, 6.0, ((0, 512),))
    norm_gain = jnp.clip(1.0 + 0.1 * jax.random.normal(key_of[5], (D,), jnp.float32), 0.5, 1.5)
    lengths = draw_lengths(jax.random.fold_in(key_of[8], 71), 0)
    owner_blocks = draw_owner_blocks(jax.random.fold_in(key_of[8], 71), 0)
    return dict(queries=queries, keys=keys, values=values, out_weight=out_weight, residual=residual, norm_gain=norm_gain, lengths=lengths, owner_blocks=owner_blocks)


FLOOR_SCORE = -1e+30

def doc_index(positions, lengths):
    ends = jnp.cumsum(lengths).astype(jnp.int32)
    return lax.optimization_barrier(jnp.sum((positions[:, None] >= ends[None, :]).astype(jnp.int32), axis=1)).astype(jnp.int32)

def reference(queries, keys, values, out_weight, residual, norm_gain, lengths, owner_blocks):
    positions = jnp.arange(SEQ, dtype=jnp.int32)
    doc = doc_index(positions, lengths)
    order = (owner_blocks.reshape(-1)[:, None] * BLOCK + jnp.arange(BLOCK, dtype=jnp.int32)[None, :]).reshape(-1).astype(jnp.int32)
    group = HEADS // KV_HEADS
    q_rows = jnp.take(queries, order, axis=0).reshape(SEQ, KV_HEADS, group, HD)
    q_doc = jnp.take(doc, order)
    key_all = keys.astype(jnp.float32).reshape(SEQ, KV_HEADS, HD)
    value_all = values.astype(jnp.float32).reshape(SEQ, KV_HEADS, HD)
    scale = 1.0 / math.sqrt(HD)
    sub_len = math.gcd(SEQ, 256)

    def one_block(block_index):
        offset = block_index * sub_len
        q_block = lax.dynamic_slice_in_dim(q_rows, offset, sub_len).astype(jnp.float32)
        pos_block = lax.dynamic_slice_in_dim(order, offset, sub_len)
        doc_block = lax.dynamic_slice_in_dim(q_doc, offset, sub_len)
        visible = (positions[None, :] <= pos_block[:, None]) & (doc[None, :] == doc_block[:, None])
        scores = jnp.einsum('qgjd,kgd->gjqk', q_block, key_all) * scale
        scores = jnp.where(visible[None, None], scores, FLOOR_SCORE)
        row_max = lax.optimization_barrier(jnp.max(scores, axis=3, keepdims=True))
        weights = jnp.where(visible[None, None], jnp.exp(scores - row_max), 0.0)
        row_sum = lax.optimization_barrier(jnp.sum(weights, axis=3))
        rounded = lax.optimization_barrier(weights.astype(jnp.bfloat16)).astype(jnp.float32)
        context = jnp.einsum('gjqk,kgd->gjqd', rounded, value_all) / row_sum[..., None]
        return jnp.transpose(context, (2, 0, 1, 3)).reshape(sub_len, HEADS * HD).astype(jnp.bfloat16)
    attended = lax.map(one_block, jnp.arange(SEQ // sub_len, dtype=jnp.int32)).reshape(SEQ, HEADS * HD)
    width_dev = HEADS_DEV * HD
    pieces = attended.reshape(SEQ, N_TP, width_dev)
    weight_parts = out_weight.reshape(N_TP, width_dev, D)

    def add_part(running, part_index):
        term = jnp.dot(pieces[:, part_index], weight_parts[part_index], preferred_element_type=jnp.float32)
        rounded = lax.optimization_barrier(term.astype(jnp.bfloat16)).astype(jnp.float32)
        return (running + rounded, None)
    projected, _ = lax.scan(add_part, jnp.zeros((SEQ, D), jnp.float32), jnp.arange(N_TP, dtype=jnp.int32))
    mean_sq = lax.optimization_barrier(jnp.mean(projected * projected, axis=1, keepdims=True))
    normed = projected * lax.rsqrt(mean_sq + 1e-06) * norm_gain.astype(jnp.float32)
    return (residual.astype(jnp.float32) + normed).astype(jnp.bfloat16)
```

```python
import functools
import math

import jax
import jax.numpy as jnp
from jax import lax
from jax.experimental import pallas as pl
from jax.experimental.pallas import tpu as pltpu
from jax.sharding import PartitionSpec as P

MESH = pl.DeviceIdType.MESH

HD = 128
BLOCK = 128
TOK = 256
SIDE = 4
CHIPS = SIDE * SIDE
CT = 2 * TOK
PLANE = 2 * CHIPS
FLOOR = -1e30
SCALE = math.log2(math.e) / math.sqrt(HD)
BF = jnp.bfloat16
F32 = jnp.float32


def iota(shape, dim):
    return lax.broadcasted_iota(jnp.int32, shape, dim)


def kernel(
    nt,
    docs,
    q_hbm,
    k_hbm,
    v_hbm,
    w_hbm,
    res_hbm,
    gain_hbm,
    len_ref,
    own_ref,
    out_ref,
    qbuf,
    vtmp,
    kv,
    qt,
    acc,
    stat,
    send1,
    recv1,
    perm,
    send2,
    abuf,
    wbuf,
    part1,
    part2,
    sib_out,
    sib_in,
    osend,
    obuf,
    resv,
    gainv,
    loc_sem,
    q_sem,
    kv_send,
    kv_recv,
    sib_send,
    sib_recv,
    w_send,
    w_recv,
    a1_send,
    a1_recv,
    z_send,
    z_recv,
    ag_send,
    ag_recv,
    x_sem,
    fin_send,
    fin_recv,
):
    ni = nt // 2
    ext = 8 // ni
    rb = ext * 32
    orows = 16 * ext
    me = lax.axis_index("ctx")
    t = lax.axis_index("tp")
    c = me // 2
    h = me % 2
    sib = (me + 1 - 2 * h, t)
    x = c % SIDE
    y = c // SIDE
    u = x + h * (y - x)
    v = y + h * (x - y)

    def chip(uu, vv):
        return (uu % SIDE) * (1 + 3 * h) + (vv % SIDE) * (4 - 3 * h)

    def remote(src, dst, ssem, rsem, dev):
        return pltpu.make_async_remote_copy(
            src_ref=src, dst_ref=dst, send_sem=ssem, recv_sem=rsem, device_id=dev, device_id_type=MESH
        )

    head = pl.multiple_of(h * HD, HD)
    other_head = pl.multiple_of((1 - h) * HD, HD)
    my_w = pl.ds(pl.multiple_of(t * HD, HD), HD)
    col1 = pl.ds(pl.multiple_of(c * 256, 256), 256)
    col2 = pl.ds(pl.multiple_of(4096 + (c // 2) * 128, 128), 128)
    loads = [
        (k_hbm, kv.at[h, c, 0]),
        (v_hbm, vtmp),
        (q_hbm.at[:, pl.ds(head, HD)], qbuf.at[h]),
        (w_hbm.at[pl.ds(head, HD), col1], wbuf.at[my_w, pl.ds(0, 256)]),
        (w_hbm.at[pl.ds(head, HD), col2], wbuf.at[my_w, pl.ds(256, 128)]),
        (res_hbm, resv),
        (gain_hbm, gainv),
    ]
    loads = [pltpu.make_async_copy(s, d, loc_sem.at[n]) for n, (s, d) in enumerate(loads)]
    for copy in loads:
        copy.start()
    barrier = pltpu.get_barrier_semaphore()

    @pl.loop(1, PLANE)
    def _(d):
        pl.semaphore_signal(barrier, inc=1, device_id=((me + d) % PLANE, t), device_id_type=MESH)

    @pl.loop(1, nt)
    def _(d):
        pl.semaphore_signal(barrier, inc=1, device_id=(me, (t + d) % nt), device_id_type=MESH)

    row = iota((CT, 1), 0)
    target = (row % 16) * 32 + (row // BLOCK) * 8 + (row % BLOCK) // 16
    spread = jnp.where(iota((CT, CT), 1) == target, 1.0, 0.0).astype(BF)
    perm[...] = spread
    lane = iota((1, CT), 1)
    pos = c * CT + ((lane // 8) % 4) * BLOCK + (lane % 8) * 16 + lane // 32
    first = jnp.zeros((1, CT), jnp.int32)
    end = jnp.int32(0)
    for n in range(docs):
        end = end + len_ref[n]
        first = jnp.where(end <= pos, end, first)

    loads[0].wait()
    loads[1].wait()
    vt = vtmp[...].astype(F32)
    for n in range(TOK // HD):
        kv[h, c, 1, n * HD : (n + 1) * HD, :] = vt[n * HD : (n + 1) * HD, :].T.astype(BF)
    loads[2].wait()
    loads[3].wait()
    loads[4].wait()

    pl.semaphore_wait(barrier, PLANE - 1 + nt - 1)

    right = (me, (t + 1) % nt)
    left = (me, (t + nt - 1) % nt)
    rsteps = nt // 2
    lsteps = nt - 1 - rsteps

    def w_copy(way, step):
        slot = (t - step + nt) % nt if way == 0 else (t + step) % nt
        ref = wbuf.at[pl.ds(pl.multiple_of(slot * HD, HD), HD)]
        return remote(ref, ref, w_send.at[way, step], w_recv.at[way, step], right if way == 0 else left)

    def w_step(step):
        for way, count in ((0, rsteps), (1, lsteps)):
            if step >= 1 and step - 1 < count:
                w_copy(way, step - 1).wait_recv()
            if step < count:
                w_copy(way, step).start()

    def w_finish():
        for way, count in ((0, rsteps), (1, lsteps)):
            for step in range(count):
                w_copy(way, step).wait_send()

    def gather(buf, ssem, rsem, on_ready, pause):
        def full(src, to, n):
            return remote(buf.at[src], buf.at[src], ssem.at[n], rsem.at[src, 0], (to * 2 + h, t))

        def half(src, part, to, n):
            ref = buf.at[src, part]
            return remote(ref, ref, ssem.at[n], rsem.at[src, part], (to * 2 + h, t))

        sends = []

        def go(copy):
            copy.start()
            sends.append(copy)

        def onward(uu, n):
            src = chip(uu, v)
            go(full(src, chip(u, v + 1), n))
            go(full(src, chip(u, v + 3), n + 1))
            on_ready(src)

        go(full(c, chip(u + 1, v), 0))
        go(full(c, chip(u + 3, v), 1))
        onward(u, 2)
        pause(0)
        low = chip(u + 3, v)
        full(low, c, 4).wait_recv()
        go(half(low, 0, chip(u + 1, v), 4))
        high = chip(u + 1, v)
        full(high, c, 5).wait_recv()
        go(half(high, 1, chip(u + 3, v), 5))
        onward(u + 3, 6)
        onward(u + 1, 8)
        pause(1)
        far = chip(u + 2, v)
        half(far, 0, c, 10).wait_recv()
        half(far, 1, c, 10).wait_recv()
        onward(u + 2, 10)
        pause(2)
        n = 12
        for du in (0, 3, 1, 2):
            low = chip(u + du, v + 3)
            full(low, c, n).wait_recv()
            go(half(low, 0, chip(u, v + 1), n))
            on_ready(low)
            high = chip(u + du, v + 1)
            full(high, c, n + 1).wait_recv()
            go(half(high, 1, chip(u, v + 3), n + 1))
            on_ready(high)
            n += 2
            if du == 3:
                pause(3)
        pause(4)
        for du in (0, 3, 1, 2):
            far = chip(u + du, v + 2)
            half(far, 0, c, 0).wait_recv()
            half(far, 1, c, 0).wait_recv()
            on_ready(far)
        for copy in sends:
            copy.wait_send()

    def attend(src, start):
        keys = jnp.concatenate([kv[0, src, 0], kv[1, src, 0]], axis=0)
        pieces = []
        for core in range(2):
            block = kv[core, src, 1]
            pieces += [block[n * HD : (n + 1) * HD] for n in range(TOK // HD)]
        values = jnp.concatenate(pieces, axis=1)
        wide = 256
        for n in range(CT // wide):
            cols = slice(n * wide, (n + 1) * wide)
            score = jnp.dot(keys, qt[:, cols], preferred_element_type=F32) * SCALE
            kpos = src * CT + iota((CT, wide), 0)
            visible = kpos >= first[:, cols]
            if start:
                visible = visible & (kpos <= pos[:, cols])
            score = jnp.where(visible, score, FLOOR)
            top = jnp.max(score, axis=0, keepdims=True)
            if not start:
                old = stat[0:1, cols]
                top = jnp.maximum(top, old)
                decay = jnp.exp2(old - top)
            weight = jnp.exp2(score - top)
            total = jnp.sum(weight, axis=0, keepdims=True)
            context = jnp.dot(values, weight.astype(BF), preferred_element_type=F32)
            if not start:
                total = total + stat[1:2, cols] * decay
                context = context + acc[:, cols] * decay
            stat[0:1, cols] = top
            stat[1:2, cols] = total
            acc[:, cols] = context

    def swap_copy(src):
        ref = kv.at[h, src]
        return remote(ref, ref, sib_send.at[src], sib_recv.at[src], sib)

    def swap_wait(src):
        ref = kv.at[1 - h, src]
        remote(ref, ref, sib_send.at[src], sib_recv.at[src], sib).wait_recv()

    q_send = remote(q_hbm.at[:, pl.ds(other_head, HD)], qbuf.at[h], q_sem.at[0], q_sem.at[1], sib)
    q_send.start()

    def kv_ready(src):
        swap_copy(src).start()

    def kv_pause(n):
        if n == 0:
            w_step(0)
            q_send.wait_recv()
            for core in range(2):
                rows = qbuf[core].astype(F32).T.astype(BF)
                some = jnp.dot(rows, perm[core * TOK : (core + 1) * TOK, :], preferred_element_type=F32)
                if core == 0:
                    total = some
                else:
                    total = total + some
            qt[...] = total.astype(BF)
            swap_wait(c)
            attend(c, True)
        elif n < 5:
            w_step(n)

    gather(kv.at[h], kv_send, kv_recv, kv_ready, kv_pause)

    @pl.loop(1, CHIPS)
    def _(d):
        swap_wait((c + d) % CHIPS)

    @pl.loop(1, jnp.minimum(c, 8) + 1)
    def _(k):
        attend(c - k, False)

    w_step(5)
    result = (acc[...] / stat[1:2, :]).T.astype(BF)
    send1[...] = result

    def a1_copy(d):
        to = (c + d) % CHIPS
        return remote(
            send1.at[pl.ds(pl.multiple_of(to * 32, 32), 32)],
            recv1.at[pl.ds(pl.multiple_of(c * 32, 32), 32)],
            a1_send.at[d],
            a1_recv.at[d],
            (to * 2 + h, t),
        )

    @pl.loop(1, CHIPS)
    def _(d):
        a1_copy(d).start()

    mine = pl.ds(pl.multiple_of(c * 32, 32), 32)
    recv1[mine, :] = send1[mine, :]

    for k in range(2):
        owned = own_ref[:, k : k + 1] * 8
        for i in range(8):
            rows = slice((k * 8 + i) * 32, (k * 8 + i + 1) * 32)
            perm[rows, :] = jnp.where(iota((32, CT), 1) == owned + i, 1.0, 0.0).astype(BF)

    @pl.loop(1, CHIPS)
    def _(d):
        a1_copy(d).wait()

    send2[...] = jnp.dot(perm[...], recv1[...], preferred_element_type=F32).astype(BF)

    def z_dst():
        return abuf.at[c, t // ni, pl.ds(pl.multiple_of((t % ni) * rb, 32), rb)]

    def z_copy(d):
        to = (t + d) % nt
        return remote(
            send2.at[pl.ds(pl.multiple_of(to * rb, 32), rb)], z_dst(), z_send.at[d], z_recv.at[d], (me, to)
        )

    @pl.loop(1, nt)
    def _(d):
        z_copy(d).start()

    abuf[c, t // ni, pl.ds(pl.multiple_of((t % ni) * rb, 32), rb), :] = send2[
        pl.ds(pl.multiple_of(t * rb, 32), rb), :
    ]
    w_step(6)

    @pl.loop(1, nt)
    def _(d):
        z_copy(d).wait()

    def ag_pause(n):
        if n == 2:
            w_step(7)
        if n == 4:
            w_step(8)

    gather(abuf, ag_send, ag_recv, lambda src: None, ag_pause)
    w_finish()

    half_of = c % 2

    @pl.loop(0, SIDE)
    def _(g):
        lhs1 = []
        lhs2 = []
        for s in range(nt):
            base = (s % ni) * rb
            lhs1.append(abuf[pl.ds(g * 4, 4), s // ni, base : base + rb, :].reshape(4 * rb, HD))
            for e in range(ext):
                at = pl.ds(pl.multiple_of(base + e * 32 + half_of * 16, 16), 16)
                lhs2.append(abuf[pl.ds(g * 4, 4), s // ni, at, :])
        lhs1 = jnp.concatenate(lhs1, axis=1)
        cat = []
        for s in range(nt):
            cat.append(jnp.concatenate(lhs2[s * ext : (s + 1) * ext], axis=1).reshape(4 * ext * 16, HD))
        lhs2 = jnp.concatenate(cat, axis=1)
        product = jnp.dot(lhs1, wbuf[:, 0:256], preferred_element_type=F32)
        for core in range(2):
            part1[core, pl.ds(pl.multiple_of(g * 4 * rb, 128), 4 * rb), :] = product[:, core * HD : (core + 1) * HD]
        part2[pl.ds(pl.multiple_of(g * 2 * rb, 64), 2 * rb), :] = jnp.dot(
            lhs2, wbuf[:, 256:384], preferred_element_type=F32
        )

    def tile(n, core):
        out = []
        for e in range(ext):
            out.append(part1[core, pl.ds(e * 32 + n, 16, stride=rb), :])
        return out

    def tile2(n, core):
        out = []
        for e in range(ext):
            out.append(part2[pl.ds(e * 16 + core * 8 + n, 16, stride=rb // 2), :])
        return out

    def exchange(put, core):
        for n in range(32):
            for e, val in enumerate(tile(n, core)):
                put(n, e, val)
        for n in range(8):
            for e, val in enumerate(tile2(n, core)):
                put(32 + n, e, val)

    def put_sib(n, e, val):
        sib_out[n, e * 16 : (e + 1) * 16, :] = val.astype(BF)

    exchange(put_sib, 1 - h)
    x_copy = remote(sib_out, sib_in, x_sem.at[0], x_sem.at[1], sib)
    x_copy.start()
    x_copy.wait()

    def put_fin(n, e, val):
        rows = slice(e * 16, (e + 1) * 16)
        osend[n, rows, :] = (val + sib_in[n, rows, :].astype(F32)).astype(BF)

    exchange(put_fin, h)

    def fin_copy(d):
        to = (me + d) % PLANE
        return remote(osend.at[to], obuf.at[me], fin_send.at[d], fin_recv.at[d], (to, t))

    @pl.loop(1, PLANE)
    def _(d):
        fin_copy(d).start()

    base = half_of * 16 + h * 8
    shared = 32 + c // 2

    def fin2_copy(n):
        return remote(
            osend.at[32 + n], obuf.at[shared], fin_send.at[PLANE + n], fin_recv.at[PLANE + c // 2], (base + n, t)
        )

    @pl.loop(0, 8)
    def _(n):
        @pl.when(base + n != me)
        def _():
            fin2_copy(n).start()

    obuf[me] = osend[me]

    @pl.when((me >= base) & (me < base + 8))
    def _():
        obuf[shared] = osend[32 + jnp.clip(me - base, 0, 7)]

    loads[5].wait()
    loads[6].wait()

    @pl.loop(1, PLANE)
    def _(d):
        fin_copy(d).wait()

    @pl.loop(0, 8)
    def _(n):
        @pl.when(base + n != me)
        def _():
            fin2_copy(n).wait_send()

        @pl.when((2 * n + me // 16) * 2 + (me % 16) // 8 != me)
        def _():
            remote(osend.at[0], obuf.at[32 + n], fin_send.at[0], fin_recv.at[PLANE + n], sib).wait_recv()

    q_send.wait_send()

    @pl.loop(0, CHIPS)
    def _(n):
        swap_copy(n).wait_send()

    square = jnp.zeros((orows, HD), F32)
    for n in range(40):
        val = obuf[n].astype(F32)
        square = square + val * val
    mean = jnp.sum(square, axis=1, keepdims=True) / (40 * HD)
    factor = lax.rsqrt(mean + 1e-6)
    for n in range(40):
        cols = slice(n * HD, (n + 1) * HD)
        val = obuf[n].astype(F32) * factor * gainv[n : n + 1, :]
        out_ref[:, cols] = (resv[:, cols].astype(F32) + val).astype(BF)


def per_device(queries, keys, values, out_weight, residual, norm_gain, lengths, owner_blocks):
    nt = lax.axis_size("tp")
    docs = lengths.shape[0]
    width = out_weight.shape[1]
    ext = 16 // nt
    orows = 16 * ext
    any_spec = pl.BlockSpec(memory_space=pl.ANY)
    vmem = pltpu.VMEM
    dma = pltpu.SemaphoreType.DMA
    scratch = dict(
        qbuf=vmem((2, TOK, HD), BF),
        vtmp=vmem((TOK, HD), BF),
        kv=vmem((2, CHIPS, 2, TOK, HD), BF),
        qt=vmem((HD, CT), BF),
        acc=vmem((HD, CT), F32),
        stat=vmem((8, CT), F32),
        send1=vmem((CT, HD), BF),
        recv1=vmem((CT, HD), BF),
        perm=vmem((CT, CT), BF),
        send2=vmem((CT, HD), BF),
        abuf=vmem((CHIPS, 2, TOK, HD), BF),
        wbuf=vmem((nt * HD, 3 * HD), BF),
        part1=vmem((2, CT * ext, HD), F32),
        part2=vmem((CT * ext // 2, HD), F32),
        sib_out=vmem((40, orows, HD), BF),
        sib_in=vmem((40, orows, HD), BF),
        osend=vmem((40, orows, HD), BF),
        obuf=vmem((40, orows, HD), BF),
        resv=vmem((orows, width), BF),
        gainv=vmem((width // HD, HD), F32),
        loc_sem=dma((7,)),
        q_sem=dma((2,)),
        kv_send=dma((20,)),
        kv_recv=dma((CHIPS, 2)),
        sib_send=dma((CHIPS,)),
        sib_recv=dma((CHIPS,)),
        w_send=dma((2, 8)),
        w_recv=dma((2, 8)),
        a1_send=dma((CHIPS,)),
        a1_recv=dma((CHIPS,)),
        z_send=dma((16,)),
        z_recv=dma((16,)),
        ag_send=dma((20,)),
        ag_recv=dma((CHIPS, 2)),
        x_sem=dma((2,)),
        fin_send=dma((PLANE + 8,)),
        fin_recv=dma((PLANE + 8,)),
    )
    return pl.pallas_call(
        functools.partial(kernel, nt, docs),
        out_shape=jax.ShapeDtypeStruct((orows, width), BF),
        in_specs=[any_spec] * 6
        + [pl.BlockSpec(memory_space=pltpu.SMEM), pl.BlockSpec(memory_space=pltpu.VMEM)],
        out_specs=pl.BlockSpec(memory_space=pltpu.VMEM),
        scratch_shapes=list(scratch.values()),
        compiler_params=pltpu.CompilerParams(
            collective_id=0, has_side_effects=True, vmem_limit_bytes=48 * 1024 * 1024
        ),
        name="attend_project",
    )(
        queries,
        keys,
        values,
        out_weight,
        residual,
        norm_gain.reshape(width // HD, HD),
        lengths,
        owner_blocks,
    )


def solution(mesh):
    in_specs = (
        P("ctx", "tp"),
        P("ctx", "tp"),
        P("ctx", "tp"),
        P("tp", None),
        P(("ctx", "tp"), None),
        P(),
        P(),
        P(),
    )
    out_specs = P(("ctx", "tp"), None)
    return jax.shard_map(
        per_device, mesh=mesh, in_specs=in_specs, out_specs=out_specs, check_vma=False
    )
```

```python
import functools
import math

import jax
import jax.numpy as jnp
from jax import lax
from jax.experimental import pallas as pl
from jax.experimental.pallas import tpu as pltpu
from jax.sharding import PartitionSpec as P

MESH = pl.DeviceIdType.MESH

HD = 128
BLOCK = 128
TOK = 256
SIDE = 4
CHIPS = SIDE * SIDE
CT = 2 * TOK
PLANE = 2 * CHIPS
FLOOR = -1e30
SCALE = math.log2(math.e) / math.sqrt(HD)
BF = jnp.bfloat16
F32 = jnp.float32


def iota(shape, dim):
    return lax.broadcasted_iota(jnp.int32, shape, dim)


def kernel(
    nt,
    docs,
    q_hbm,
    k_hbm,
    v_hbm,
    w_hbm,
    res_hbm,
    gain_hbm,
    len_ref,
    own_ref,
    out_ref,
    qbuf,
    vtmp,
    kv,
    qt,
    acc,
    stat,
    send1,
    recv1,
    perm,
    perm2,
    send2,
    abuf,
    wbuf,
    part,
    xout,
    xin,
    osend,
    obuf,
    resv,
    gainv,
    hail_sem,
    loc_sem,
    q_sem,
    kv_send,
    fwd_send,
    kv_recv,
    sib_send,
    sib_recv,
    w_send,
    w_recv,
    a1_send,
    a1_recv,
    z_send,
    z_recv,
    ag_send,
    ag_recv,
    x_send,
    x_recv,
    fin_send,
    fin_recv,
):
    orows = out_ref.shape[0]
    me = lax.axis_index("ctx")
    t = lax.axis_index("tp")
    c = me // 2
    h = me % 2
    sib = (me + 1 - 2 * h, t)
    x = c % SIDE
    y = c // SIDE
    u = x + h * (y - x)
    v = y + h * (x - y)

    def chip(uu, vv):
        return (uu % SIDE) * (1 + 3 * h) + (vv % SIDE) * (4 - 3 * h)

    def remote(src, dst, ssem, rsem, dev):
        return pltpu.make_async_remote_copy(
            src_ref=src, dst_ref=dst, send_sem=ssem, recv_sem=rsem, device_id=dev, device_id_type=MESH
        )

    head = pl.multiple_of(h * HD, HD)
    other_head = pl.multiple_of((1 - h) * HD, HD)
    my_w = pl.ds(pl.multiple_of(t * HD, HD), HD)
    col1 = pl.ds(pl.multiple_of(c * 256, 256), 256)
    col2 = pl.ds(pl.multiple_of(4096 + (c // 2) * 128, 128), 128)
    loads = [
        (k_hbm, kv.at[h, c, 0]),
        (v_hbm, vtmp),
        (q_hbm.at[:, pl.ds(head, HD)], qbuf.at[h]),
        (w_hbm.at[pl.ds(head, HD), col1], wbuf.at[my_w, pl.ds(0, 256)]),
        (w_hbm.at[pl.ds(head, HD), col2], wbuf.at[my_w, pl.ds(256, 128)]),
        (res_hbm, resv),
        (gain_hbm, gainv),
    ]
    loads = [pltpu.make_async_copy(s, d, loc_sem.at[n]) for n, (s, d) in enumerate(loads)]
    for copy in loads:
        copy.start()
    barrier = pltpu.get_barrier_semaphore()

    @pl.loop(1, CHIPS)
    def _(d):
        pl.semaphore_signal(barrier, inc=1, device_id=((me + 2 * d) % PLANE, t), device_id_type=MESH)

    right = (me, (t + 1) % nt)
    left = (me, (t + nt - 1) % nt)
    for dev in (right, left, sib):
        pl.semaphore_signal(barrier, inc=1, device_id=dev, device_id_type=MESH)

    row = iota((CT, 1), 0)
    target = (row % 16) * 32 + (row // BLOCK) * 8 + (row % BLOCK) // 16
    spread = jnp.where(iota((CT, CT), 1) == target, 1.0, 0.0).astype(BF)
    perm[...] = spread
    lane = iota((1, CT), 1)
    pos = c * CT + ((lane // 8) % 4) * BLOCK + (lane % 8) * 16 + lane // 32
    first = jnp.zeros((1, CT), jnp.int32)
    end = jnp.int32(0)
    for n in range(docs):
        end = end + len_ref[n]
        first = jnp.where(end <= pos, end, first)

    for k in range(2):
        owned = jnp.zeros((PLANE, 1), jnp.int32)
        for o in range(PLANE):
            owned = jnp.where(iota((PLANE, 1), 0) == o, own_ref[k, o] * 8, owned)
        for i in range(8):
            rows = slice((k * 8 + i) * PLANE, (k * 8 + i + 1) * PLANE)
            perm2[rows, :] = jnp.where(iota((PLANE, CT), 1) == owned + i, 1.0, 0.0).astype(BF)

    loads[0].wait()
    loads[1].wait()
    vt = vtmp[...].astype(F32)
    for n in range(TOK // HD):
        kv[h, c, 1, n * HD : (n + 1) * HD, :] = vt[n * HD : (n + 1) * HD, :].T.astype(BF)
    loads[2].wait()
    loads[3].wait()
    loads[4].wait()

    pl.semaphore_wait(barrier, CHIPS + 2)

    def hail(n):
        for dev in ((me, (t + 2**n) % nt), (me, (t + nt - 2**n) % nt)):
            pl.semaphore_signal(hail_sem.at[n], inc=1, device_id=dev, device_id_type=MESH)

    def heard(n):
        pl.semaphore_wait(hail_sem.at[n], 2)

    hail(0)

    rsteps = nt // 2
    lsteps = nt - 1 - rsteps

    def w_copy(way, step):
        slot = (t - step + nt) % nt if way == 0 else (t + step) % nt
        ref = wbuf.at[pl.ds(pl.multiple_of(slot * HD, HD), HD)]
        return remote(ref, ref, w_send.at[way, step], w_recv.at[way, step], right if way == 0 else left)

    def w_step(step):
        for way, count in ((0, rsteps), (1, lsteps)):
            if step >= 1 and step - 1 < count:
                w_copy(way, step - 1).wait_recv()
            if step < count:
                w_copy(way, step).start()

    def w_finish():
        for way, count in ((0, rsteps), (1, lsteps)):
            for step in range(count):
                w_copy(way, step).wait_send()

    def gather(buf, ssem, rsem, pause):
        def hop(uu, du, dv, n):
            src = chip(uu, v)
            return remote(buf.at[src], buf.at[src], ssem.at[n], rsem.at[src], (chip(u + du, v + dv) * 2 + h, t))

        def arrived(src):
            remote(buf.at[src], buf.at[src], ssem.at[0], rsem.at[src], sib).wait_recv()

        sends = [hop(u, d, 0, n) for n, d in enumerate((1, 3, 2))]
        sends += [hop(u, 0, d, 3 + n) for n, d in enumerate((1, 3, 2))]
        for copy in sends:
            copy.start()
        pause(0)
        for m, du in enumerate((1, 3, 2)):
            arrived(chip(u + du, v))
            for n, d in enumerate((1, 3, 2)):
                copy = hop(u + du, 0, d, 6 + 3 * m + n)
                copy.start()
                sends.append(copy)
        pause(1)
        for m, du in enumerate((0, 1, 3, 2)):
            for dv in (1, 3, 2):
                arrived(chip(u + du, v + dv))
            pause(2 + m)
        for copy in sends:
            copy.wait_send()

    def attend(src, start):
        keys = jnp.concatenate([kv[0, src, 0], kv[1, src, 0]], axis=0)
        pieces = []
        for core in range(2):
            block = kv[core, src, 1]
            pieces += [block[n * HD : (n + 1) * HD] for n in range(TOK // HD)]
        values = jnp.concatenate(pieces, axis=1)
        wide = 256
        for n in range(CT // wide):
            cols = slice(n * wide, (n + 1) * wide)
            score = jnp.dot(keys, qt[:, cols], preferred_element_type=F32) * SCALE
            kpos = src * CT + iota((CT, wide), 0)
            visible = kpos >= first[:, cols]
            if start:
                visible = visible & (kpos <= pos[:, cols])
            score = jnp.where(visible, score, FLOOR)
            top = jnp.max(score, axis=0, keepdims=True)
            if not start:
                old = stat[0:1, cols]
                top = jnp.maximum(top, old)
                decay = jnp.exp2(old - top)
            weight = jnp.exp2(score - top)
            total = jnp.sum(weight, axis=0, keepdims=True)
            context = jnp.dot(values, weight.astype(BF), preferred_element_type=F32)
            if not start:
                total = total + stat[1:2, cols] * decay
                context = context + acc[:, cols] * decay
            stat[0:1, cols] = top
            stat[1:2, cols] = total
            acc[:, cols] = context

    def swap_copy(src):
        ref = kv.at[h, src]
        return remote(ref, ref, sib_send.at[src], sib_recv.at[src], sib)

    def swap_wait(src):
        ref = kv.at[1 - h, src]
        remote(ref, ref, sib_send.at[src], sib_recv.at[src], sib).wait_recv()

    q_send = remote(q_hbm.at[:, pl.ds(other_head, HD)], qbuf.at[h], q_sem.at[0], q_sem.at[1], sib)
    q_send.start()

    def kv_copy(src, ssem, to):
        ref = kv.at[h, src]
        return remote(ref, ref, ssem, kv_recv.at[to - src], (to * 2 + h, t))

    own_sends = [(4, y < 3), (8, y < 2), (1, x < 3), (2, x < 2), (3, x < 1)]

    def forwards(dy):
        for dx in range(1, SIDE):
            to = y * SIDE + (x + dx) % SIDE
            yield kv_copy(c - 4 * dy, fwd_send.at[dy - 1, dx - 1], to), (y >= dy) & ((dy == 1) | (x + dx >= SIDE))

    for k, cond in own_sends:

        @pl.when(cond)
        def _():
            kv_copy(c, kv_send.at[k], c + k).start()

    swap_copy(c).start()
    w_step(0)
    q_send.wait_recv()
    for core in range(2):
        rows = qbuf[core].astype(F32).T.astype(BF)
        some = jnp.dot(rows, perm[core * TOK : (core + 1) * TOK, :], preferred_element_type=F32)
        if core == 0:
            total = some
        else:
            total = total + some
    qt[...] = total.astype(BF)
    heard(0)
    hail(1)
    swap_wait(c)
    attend(c, True)

    for dy in (1, 2):

        @pl.when(y >= dy)
        def _():
            kv_copy(c - 4 * dy, kv_send.at[0], c).wait_recv()

        for copy, cond in forwards(dy):

            @pl.when(cond)
            def _():
                copy.start()

    heard(1)
    hail(2)

    reach = jnp.minimum(c, 8)

    @pl.loop(1, reach + 2)
    def _(k):
        @pl.when(k <= reach)
        def _():
            @pl.when(k % 4 > 0)
            def _():
                kv_copy(c - k, kv_send.at[0], c).wait_recv()

            swap_copy(c - k).start()

        @pl.when(k >= 2)
        def _():
            swap_wait(c - k + 1)
            attend(c - k + 1, False)

        for step, at in ((1, 2), (2, 5), (3, 8)):

            @pl.when(k == at)
            def _():
                w_step(step)

    for step, at in ((1, 2), (2, 5), (3, 8)):

        @pl.when(reach + 1 < at)
        def _():
            w_step(step)

    w_step(4)
    result = (acc[...] / stat[1:2, :]).T.astype(BF)
    send1[...] = result

    def a1_copy(d):
        to = (c + d) % CHIPS
        return remote(
            send1.at[pl.ds(pl.multiple_of(to * 32, 32), 32)],
            recv1.at[pl.ds(pl.multiple_of(c * 32, 32), 32)],
            a1_send.at[d],
            a1_recv.at[d],
            (to * 2 + h, t),
        )

    @pl.loop(1, CHIPS)
    def _(d):
        a1_copy(d).start()

    mine = pl.ds(pl.multiple_of(c * 32, 32), 32)
    recv1[mine, :] = send1[mine, :]

    @pl.loop(1, CHIPS)
    def _(d):
        a1_copy(d).wait()


    send2[...] = jnp.dot(perm2[...], recv1[...], preferred_element_type=F32).astype(BF)

    heard(2)

    def z_copy(d):
        to = (t + d) % nt
        return remote(
            send2.at[pl.ds(pl.multiple_of(to * 32, 32), 32)], abuf.at[c, t], z_send.at[d], z_recv.at[d], (me, to)
        )

    @pl.loop(0, nt - 1)
    def _(n):
        z_copy((nt // 2 + (n + 1) // 2 * (1 - 2 * (n % 2))) % nt).start()

    abuf[c, t] = send2[pl.ds(pl.multiple_of(t * 32, 32), 32), :]
    w_step(5)

    @pl.loop(1, nt)
    def _(d):
        z_copy(d).wait()

    half_of = c % 2

    def x_copy(a):
        rows = pl.ds(pl.multiple_of(a * 48, 16), 48)
        return remote(xout.at[rows], xin.at[rows], x_send.at[a], x_recv.at[a], sib)

    def product(chips):
        lhs1 = []
        lhs2 = []
        shared_rows = pl.ds(pl.multiple_of(half_of * 16, 16), 16)
        for s in range(nt):
            lhs1.append(jnp.concatenate([abuf[a, s] for a in chips], axis=0))
            lhs2.append(jnp.concatenate([abuf[a, s, shared_rows, :] for a in chips], axis=0))
        full = jnp.dot(jnp.concatenate(lhs1, axis=1), wbuf[:, 0:256], preferred_element_type=F32)
        some = jnp.dot(jnp.concatenate(lhs2, axis=1), wbuf[:, 256:384], preferred_element_type=F32)
        first_tile = full[:, 0:HD]
        second_tile = full[:, HD:]
        mine = jnp.where(h == 0, first_tile, second_tile)
        other = jnp.where(h == 0, second_tile, first_tile)
        for n, a in enumerate(chips):
            at = pl.multiple_of(a * 48, 16)
            part[pl.ds(at, 32), :] = mine[n * 32 : (n + 1) * 32]
            part[pl.ds(at + 32, 16), :] = some[n * 16 : (n + 1) * 16]
            xout[pl.ds(at, 32), :] = other[n * 32 : (n + 1) * 32]
            xout[pl.ds(at + 32, 16), :] = some[n * 16 : (n + 1) * 16]
            x_copy(a).start()

    def ag_pause(n):
        if n == 0:
            w_step(6)
        if n == 1:
            w_step(7)
            w_step(8)
            w_finish()
        if n >= 2:
            product([chip(u + (0, 1, 3, 2)[n - 2], v + dv) for dv in range(SIDE)])

    gather(abuf, ag_send, ag_recv, ag_pause)

    @pl.loop(0, CHIPS)
    def _(a):
        x_copy(a).wait()

    for n in range(40):
        base = n if n < 32 else 32 + h * 8 + n - 32
        rows = pl.ds(base, 16, stride=48)
        osend[n] = (part[rows, :] + xin[rows, :]).astype(BF)

    def fin_copy(d):
        to = (me + d) % PLANE
        return remote(osend.at[to], obuf.at[me], fin_send.at[d], fin_recv.at[d], (to, t))

    @pl.loop(1, PLANE)
    def _(d):
        fin_copy(d).start()

    base = half_of * 16 + h * 8
    shared = 32 + c // 2

    def fin2_copy(n):
        return remote(
            osend.at[32 + n], obuf.at[shared], fin_send.at[PLANE + n], fin_recv.at[PLANE + c // 2], (base + n, t)
        )

    @pl.loop(0, 8)
    def _(n):
        @pl.when(base + n != me)
        def _():
            fin2_copy(n).start()

    obuf[me] = osend[me]

    @pl.when((me >= base) & (me < base + 8))
    def _():
        obuf[shared] = osend[32 + jnp.clip(me - base, 0, 7)]

    loads[5].wait()
    loads[6].wait()

    @pl.loop(1, PLANE)
    def _(d):
        fin_copy(d).wait()

    @pl.loop(0, 8)
    def _(n):
        @pl.when(base + n != me)
        def _():
            fin2_copy(n).wait_send()

        @pl.when((2 * n + me // 16) * 2 + (me % 16) // 8 != me)
        def _():
            remote(osend.at[0], obuf.at[32 + n], fin_send.at[0], fin_recv.at[PLANE + n], sib).wait_recv()

    q_send.wait_send()

    @pl.loop(0, reach + 1)
    def _(k):
        swap_copy(c - k).wait_send()

    for k, cond in own_sends:

        @pl.when(cond)
        def _():
            kv_copy(c, kv_send.at[k], c + k).wait_send()

    for dy in (1, 2):
        for copy, cond in forwards(dy):

            @pl.when(cond)
            def _():
                copy.wait_send()

    square = jnp.zeros((orows, HD), F32)
    for n in range(40):
        val = obuf[n].astype(F32)
        square = square + val * val
    mean = jnp.sum(square, axis=1, keepdims=True) / (40 * HD)
    factor = lax.rsqrt(mean + 1e-6)
    for n in range(40):
        cols = slice(n * HD, (n + 1) * HD)
        val = obuf[n].astype(F32) * factor * gainv[n : n + 1, :]
        out_ref[:, cols] = (resv[:, cols].astype(F32) + val).astype(BF)


def per_device(queries, keys, values, out_weight, residual, norm_gain, lengths, owner_blocks):
    nt = lax.axis_size("tp")
    docs = lengths.shape[0]
    width = out_weight.shape[1]
    orows = residual.shape[0]
    any_spec = pl.BlockSpec(memory_space=pl.ANY)
    vmem = pltpu.VMEM
    dma = pltpu.SemaphoreType.DMA
    scratch = dict(
        qbuf=vmem((2, TOK, HD), BF),
        vtmp=vmem((TOK, HD), BF),
        kv=vmem((2, CHIPS, 2, TOK, HD), BF),
        qt=vmem((HD, CT), BF),
        acc=vmem((HD, CT), F32),
        stat=vmem((8, CT), F32),
        send1=vmem((CT, HD), BF),
        recv1=vmem((CT, HD), BF),
        perm=vmem((CT, CT), BF),
        perm2=vmem((CT, CT), BF),
        send2=vmem((CT, HD), BF),
        abuf=vmem((CHIPS, nt, 32, HD), BF),
        wbuf=vmem((nt * HD, 3 * HD), BF),
        part=vmem((CHIPS * 48, HD), F32),
        xout=vmem((CHIPS * 48, HD), F32),
        xin=vmem((CHIPS * 48, HD), F32),
        osend=vmem((40, orows, HD), BF),
        obuf=vmem((40, orows, HD), BF),
        resv=vmem((orows, width), BF),
        gainv=vmem((width // HD, HD), F32),
        hail_sem=pltpu.SemaphoreType.REGULAR((3,)),
        loc_sem=dma((7,)),
        q_sem=dma((2,)),
        kv_send=dma((9,)),
        fwd_send=dma((2, 3)),
        kv_recv=dma((9,)),
        sib_send=dma((CHIPS,)),
        sib_recv=dma((CHIPS,)),
        w_send=dma((2, 8)),
        w_recv=dma((2, 8)),
        a1_send=dma((CHIPS,)),
        a1_recv=dma((CHIPS,)),
        z_send=dma((16,)),
        z_recv=dma((16,)),
        ag_send=dma((15,)),
        ag_recv=dma((CHIPS,)),
        x_send=dma((CHIPS,)),
        x_recv=dma((CHIPS,)),
        fin_send=dma((PLANE + 8,)),
        fin_recv=dma((PLANE + 8,)),
    )
    return pl.pallas_call(
        functools.partial(kernel, nt, docs),
        out_shape=jax.ShapeDtypeStruct((orows, width), BF),
        in_specs=[any_spec] * 6
        + [pl.BlockSpec(memory_space=pltpu.SMEM)] * 2,
        out_specs=pl.BlockSpec(memory_space=pltpu.VMEM),
        scratch_shapes=list(scratch.values()),
        compiler_params=pltpu.CompilerParams(
            collective_id=0, has_side_effects=True, vmem_limit_bytes=60 * 1024 * 1024
        ),
        name="attend_project",
    )(
        queries,
        keys,
        values,
        out_weight,
        residual,
        norm_gain.reshape(width // HD, HD),
        lengths,
        owner_blocks.T,
    )


def solution(mesh):
    in_specs = (
        P("ctx", "tp"),
        P("ctx", "tp"),
        P("ctx", "tp"),
        P("tp", None),
        P(("ctx", "tp"), None),
        P(),
        P(),
        P(),
    )
    out_specs = P(("ctx", "tp"), None)
    return jax.shard_map(
        per_device, mesh=mesh, in_specs=in_specs, out_specs=out_specs, check_vma=False
    )
```

```python
import functools
import math

import jax
import jax.numpy as jnp
from jax import lax
from jax.experimental import pallas as pl
from jax.experimental.pallas import tpu as pltpu
from jax.sharding import PartitionSpec as P

MESH = pl.DeviceIdType.MESH

HD = 128
BLOCK = 128
TOK = 256
SIDE = 4
CHIPS = SIDE * SIDE
CT = 2 * TOK
PLANE = 2 * CHIPS
TILES = 5
WIDE = TILES * HD
FLOOR = -1e30
SCALE = math.log2(math.e) / math.sqrt(HD)
BF = jnp.bfloat16
F32 = jnp.float32


def iota(shape, dim):
    return lax.broadcasted_iota(jnp.int32, shape, dim)


def kernel(
    nt,
    docs,
    q_hbm,
    k_hbm,
    v_hbm,
    w_hbm,
    res_hbm,
    gain_hbm,
    len_ref,
    own_ref,
    out_ref,
    qbuf,
    vtmp,
    kv,
    qt,
    acc,
    stat,
    send1,
    recv1,
    perm,
    perm2,
    send2,
    abuf,
    wbuf,
    part,
    osend,
    obuf,
    pick,
    proj,
    resv,
    gainv,
    hail_sem,
    loc_sem,
    q_sem,
    kv_send,
    fwd_send,
    kv_recv,
    sib_send,
    sib_recv,
    w_send,
    w_recv,
    wv_send,
    wv_recv,
    a1_send,
    a1_recv,
    z_send,
    z_recv,
    ag_send,
    ag_recv,
    fin_send,
    fin_recv,
):
    orows = out_ref.shape[0]
    me = lax.axis_index("ctx")
    t = lax.axis_index("tp")
    c = me // 2
    h = me % 2
    sib = (me + 1 - 2 * h, t)
    x = c % SIDE
    y = c // SIDE
    u = x + h * (y - x)
    v = y + h * (x - y)

    def chip(uu, vv):
        return (uu % SIDE) * (1 + 3 * h) + (vv % SIDE) * (4 - 3 * h)

    def remote(src, dst, ssem, rsem, dev):
        return pltpu.make_async_remote_copy(
            src_ref=src, dst_ref=dst, send_sem=ssem, recv_sem=rsem, device_id=dev, device_id_type=MESH
        )

    head = pl.multiple_of(h * HD, HD)
    other_head = pl.multiple_of((1 - h) * HD, HD)
    HERE = nt // 4
    low, high = v % 2, v // 2
    w_rows = pl.ds(pl.multiple_of(h * HD + low * 64, 64), 64)
    w_cols = pl.ds(pl.multiple_of((u * 2 + high) * WIDE, HD), WIDE)
    loads = [
        (k_hbm, kv.at[h, c, 0]),
        (v_hbm, vtmp),
        (q_hbm.at[:, pl.ds(head, HD)], qbuf.at[h]),
        (w_hbm.at[w_rows, w_cols], wbuf.at[HERE, low]),
        (res_hbm, resv),
        (gain_hbm, gainv),
    ]
    loads = [pltpu.make_async_copy(s, d, loc_sem.at[n]) for n, (s, d) in enumerate(loads)]
    for copy in loads:
        copy.start()
    barrier = pltpu.get_barrier_semaphore()

    @pl.loop(1, CHIPS)
    def _(d):
        pl.semaphore_signal(barrier, inc=1, device_id=((me + 2 * d) % PLANE, t), device_id_type=MESH)

    right = (me, (t + 1) % nt)
    left = (me, (t + nt - 1) % nt)
    for dev in (right, left, sib):
        pl.semaphore_signal(barrier, inc=1, device_id=dev, device_id_type=MESH)

    row = iota((CT, 1), 0)
    target = (row % 16) * 32 + (row // BLOCK) * 8 + (row % BLOCK) // 16
    spread = jnp.where(iota((CT, CT), 1) == target, 1.0, 0.0).astype(BF)
    perm[...] = spread
    lane = iota((1, CT), 1)
    pos = c * CT + ((lane // 8) % 4) * BLOCK + (lane % 8) * 16 + lane // 32
    first = jnp.zeros((1, CT), jnp.int32)
    end = jnp.int32(0)
    for n in range(docs):
        end = end + len_ref[n]
        first = jnp.where(end <= pos, end, first)

    for k in range(2):
        owned = jnp.zeros((PLANE, 1), jnp.int32)
        for o in range(PLANE):
            owned = jnp.where(iota((PLANE, 1), 0) == o, own_ref[k, o] * 8, owned)
        for i in range(8):
            rows = slice((k * 8 + i) * PLANE, (k * 8 + i + 1) * PLANE)
            perm2[rows, :] = jnp.where(iota((PLANE, CT), 1) == owned + i, 1.0, 0.0).astype(BF)

    row = iota((TILES * 16, 1), 0)
    tile_of = row // 16
    chip_of = row % 16
    lane = iota((TILES * 16, 192), 1)

    def place(uu, vv):
        return (vv % 2) * 48 + tile_of * 8 + (vv // 2) * 4 + uu

    picked = (lane == place(chip_of % 4, chip_of // 4)) | (lane == 96 + place(chip_of // 4, chip_of % 4))
    pick[...] = jnp.where(picked, 1.0, 0.0).astype(BF)
    part[2 * WIDE :, :] = jnp.zeros((256, HD), F32)

    loads[0].wait()
    loads[1].wait()
    vt = vtmp[...].astype(F32)
    for n in range(TOK // HD):
        kv[h, c, 1, n * HD : (n + 1) * HD, :] = vt[n * HD : (n + 1) * HD, :].T.astype(BF)
    loads[2].wait()
    loads[3].wait()

    pl.semaphore_wait(barrier, CHIPS + 2)

    def hail(n):
        for dev in ((me, (t + 2**n) % nt), (me, (t + nt - 2**n) % nt)):
            pl.semaphore_signal(hail_sem.at[n], inc=1, device_id=dev, device_id_type=MESH)

    def heard(n):
        pl.semaphore_wait(hail_sem.at[n], 2)

    hail(0)

    rsteps = nt // 2
    lsteps = nt - 1 - rsteps

    def w_copy(way, step):
        sign = 1 if way else -1
        src = wbuf.at[(HERE + sign * step) % nt, low]
        dst = wbuf.at[(HERE + sign * (step + 1)) % nt, low]
        return remote(src, dst, w_send.at[way, step], w_recv.at[way, step], left if way else right)

    def w_spread(slot):
        ref = wbuf.at[slot, low]
        return remote(ref, ref, wv_send.at[slot], wv_recv.at[slot], (chip(u, v + 1 - 2 * low) * 2 + h, t))

    def w_step(step):
        for way, count in ((0, rsteps), (1, lsteps)):
            if step >= 1 and step - 1 < count:
                w_copy(way, step - 1).wait_recv()
            if step < count:
                w_copy(way, step).start()

    def w_share(step):
        for way, count in ((0, rsteps), (1, lsteps)):
            if (step >= 1 and step - 1 < count) or (step == 0 and way == 0):
                w_spread((HERE + (1 if way else -1) * step) % nt).start()

    def w_finish():
        for way, count in ((0, rsteps), (1, lsteps)):
            for step in range(count):
                w_copy(way, step).wait_send()
        for slot in range(nt):
            w_spread(slot).wait_send()

    def w_arrived(slots):
        for slot in slots:
            ref = wbuf.at[slot, 1 - low]
            remote(ref, ref, wv_send.at[slot], wv_recv.at[slot], sib).wait_recv()

    def attend(src, start):
        keys = jnp.concatenate([kv[0, src, 0], kv[1, src, 0]], axis=0)
        pieces = []
        for core in range(2):
            block = kv[core, src, 1]
            pieces += [block[n * HD : (n + 1) * HD] for n in range(TOK // HD)]
        values = jnp.concatenate(pieces, axis=1)
        wide = 256
        for n in range(CT // wide):
            cols = slice(n * wide, (n + 1) * wide)
            score = jnp.dot(keys, qt[:, cols], preferred_element_type=F32) * SCALE
            kpos = src * CT + iota((CT, wide), 0)
            visible = kpos >= first[:, cols]
            if start:
                visible = visible & (kpos <= pos[:, cols])
            score = jnp.where(visible, score, FLOOR)
            top = jnp.max(score, axis=0, keepdims=True)
            if not start:
                old = stat[0:1, cols]
                top = jnp.maximum(top, old)
                decay = jnp.exp2(old - top)
            weight = jnp.exp2(score - top)
            total = jnp.sum(weight, axis=0, keepdims=True)
            context = jnp.dot(values, weight.astype(BF), preferred_element_type=F32)
            if not start:
                total = total + stat[1:2, cols] * decay
                context = context + acc[:, cols] * decay
            stat[0:1, cols] = top
            stat[1:2, cols] = total
            acc[:, cols] = context

    def swap_copy(src):
        ref = kv.at[h, src]
        return remote(ref, ref, sib_send.at[src], sib_recv.at[src], sib)

    def swap_wait(src):
        ref = kv.at[1 - h, src]
        remote(ref, ref, sib_send.at[src], sib_recv.at[src], sib).wait_recv()

    q_send = remote(q_hbm.at[:, pl.ds(other_head, HD)], qbuf.at[h], q_sem.at[0], q_sem.at[1], sib)
    q_send.start()

    def kv_copy(src, ssem, to):
        ref = kv.at[h, src]
        return remote(ref, ref, ssem, kv_recv.at[to - src], (to * 2 + h, t))

    own_sends = [(4, y < 3), (8, y < 2), (1, x < 3), (2, x < 2), (3, x < 1)]

    def forwards(dy):
        for dx in range(1, SIDE):
            to = y * SIDE + (x + dx) % SIDE
            yield kv_copy(c - 4 * dy, fwd_send.at[dy - 1, dx - 1], to), (y >= dy) & ((dy == 1) | (x + dx >= SIDE))

    for k, cond in own_sends:

        @pl.when(cond)
        def _():
            kv_copy(c, kv_send.at[k], c + k).start()

    swap_copy(c).start()
    w_step(0)
    q_send.wait_recv()
    for core in range(2):
        rows = qbuf[core].astype(F32).T.astype(BF)
        some = jnp.dot(rows, perm[core * TOK : (core + 1) * TOK, :], preferred_element_type=F32)
        if core == 0:
            total = some
        else:
            total = total + some
    qt[...] = total.astype(BF)
    heard(0)
    hail(1)
    swap_wait(c)
    attend(c, True)

    w_step(1)

    for dy in (1, 2):

        @pl.when(y >= dy)
        def _():
            kv_copy(c - 4 * dy, kv_send.at[0], c).wait_recv()

        for copy, cond in forwards(dy):

            @pl.when(cond)
            def _():
                copy.start()

    w_share(0)
    w_share(1)
    heard(1)
    hail(2)

    reach = jnp.minimum(c, 8)

    @pl.loop(1, reach + 2)
    def _(k):
        @pl.when(k <= reach)
        def _():
            @pl.when(k % 4 > 0)
            def _():
                kv_copy(c - k, kv_send.at[0], c).wait_recv()

            swap_copy(c - k).start()

        @pl.when(k >= 2)
        def _():
            swap_wait(c - k + 1)
            attend(c - k + 1, False)

        for step, at in ((2, 4), (3, 7)):

            @pl.when(k == at)
            def _():
                w_step(step)
                w_share(step)

    for step, at in ((2, 4), (3, 7)):

        @pl.when(reach + 1 < at)
        def _():
            w_step(step)
            w_share(step)

    w_step(4)
    result = (acc[...] / stat[1:2, :]).T.astype(BF)
    send1[...] = result

    def a1_copy(d):
        to = (c + d) % CHIPS
        return remote(
            send1.at[pl.ds(pl.multiple_of(to * 32, 32), 32)],
            recv1.at[pl.ds(pl.multiple_of(c * 32, 32), 32)],
            a1_send.at[d],
            a1_recv.at[d],
            (to * 2 + h, t),
        )

    def outward(n, size):
        return (size // 2 + (n + 1) // 2 * (1 - 2 * (n % 2))) % size

    @pl.loop(0, CHIPS - 1)
    def _(n):
        a1_copy(outward(n, CHIPS)).start()

    w_share(4)
    w_step(5)
    w_share(5)
    mine = pl.ds(pl.multiple_of(c * 32, 32), 32)
    recv1[mine, :] = send1[mine, :]

    @pl.loop(1, CHIPS)
    def _(d):
        a1_copy(d).wait()


    send2[...] = jnp.dot(perm2[...], recv1[...], preferred_element_type=F32).astype(BF)

    heard(2)

    def z_copy(d):
        to = (t + d) % nt
        return remote(
            send2.at[pl.ds(pl.multiple_of(to * 32, 32), 32)],
            abuf.at[high, u, (HERE - d + nt) % nt],
            z_send.at[d],
            z_recv.at[d],
            (me, to),
        )

    @pl.loop(0, nt - 1)
    def _(n):
        z_copy(outward(n, nt)).start()

    abuf[high, u, HERE] = send2[pl.ds(pl.multiple_of(t * 32, 32), 32), :]
    w_step(6)
    w_share(6)

    lower = nt // 2

    def ag_copy(own, du, side):
        at = high if own == 0 else 1 - high
        ref = abuf.at[at, u, pl.ds(side * lower, lower)]
        to = chip(u, v + 2) if du == 0 else chip(u + du, v)
        return remote(ref, ref, ag_send.at[own, side, du], ag_recv.at[at, u, side], (to * 2 + h, t))

    def ag_arrived(own, du, side):
        at = high if own == 0 else 1 - high
        uu = (u + du) % SIDE
        ref = abuf.at[at, uu, pl.ds(side * lower, lower)]
        remote(ref, ref, ag_send.at[0, 0, 0], ag_recv.at[at, uu, side], sib).wait_recv()

    def ag_all(side):
        for own in (0, 1):
            for du in (1, 3, 2):
                ag_arrived(own, du, side)

    def ag_onward(side):
        ag_arrived(1, 0, side)
        for du in (2, 1, 3):
            ag_copy(1, du, side).start()

    def product(side):
        lhs = [abuf[:, :, side * lower + n].reshape(2 * SIDE * 32, HD) for n in range(lower)]
        lhs = jnp.concatenate(lhs, axis=1)
        for first_tile in range(0, TILES, 2):
            tiles = min(2, TILES - first_tile)
            rhs = wbuf[side * lower : (side + 1) * lower, :, :, first_tile * HD : (first_tile + tiles) * HD]
            val = jnp.dot(lhs, rhs.reshape(lower * HD, tiles * HD), preferred_element_type=F32)
            for m in range(tiles):
                rows = slice((first_tile + m) * 256, (first_tile + m + 1) * 256)
                piece = val[:, m * HD : (m + 1) * HD]
                part[rows, :] = piece if side == 0 else part[rows, :] + piece

    @pl.loop(1, nt)
    def _(d):
        @pl.when((d <= HERE) | (d > nt - HERE))
        def _():
            z_copy(d).wait()

    for du in (0, 2, 1, 3):
        ag_copy(0, du, 0).start()
    w_step(7)
    w_share(7)

    @pl.loop(1, nt)
    def _(d):
        @pl.when((d > HERE) & (d <= nt - HERE))
        def _():
            z_copy(d).wait()

    for du in (0, 2, 1, 3):
        ag_copy(0, du, 1).start()
    ag_onward(0)
    w_step(8)
    w_share(8)
    ag_onward(1)
    ag_all(0)
    w_arrived(range(lower))
    product(0)
    ag_all(1)
    w_arrived(range(lower, nt))
    product(1)

    for o in range(PLANE):
        osend[o] = part[pl.ds(o, 48, stride=32), :].astype(BF)

    mine = (h * SIDE + u) * SIDE + v

    def fin_copy(d):
        to = (me + d) % PLANE
        return remote(osend.at[to], obuf.at[mine], fin_send.at[d], fin_recv.at[d], (to, t))

    @pl.loop(1, PLANE)
    def _(d):
        fin_copy(outward(d - 1, PLANE)).start()

    obuf[mine] = osend[me]
    loads[4].wait()
    loads[5].wait()
    w_finish()
    for own, du in ((0, 0), (0, 1), (0, 2), (0, 3), (1, 1), (1, 2), (1, 3)):
        for side in range(2):
            ag_copy(own, du, side).wait_send()

    q_send.wait_send()

    @pl.loop(0, reach + 1)
    def _(k):
        swap_copy(c - k).wait_send()

    for k, cond in own_sends:

        @pl.when(cond)
        def _():
            kv_copy(c, kv_send.at[k], c + k).wait_send()

    for dy in (1, 2):
        for copy, cond in forwards(dy):

            @pl.when(cond)
            def _():
                copy.wait_send()

    @pl.loop(1, PLANE)
    def _(d):
        fin_copy(d).wait()

    square = jnp.zeros((orows, HD), F32)
    for g in range(2 * SIDE):
        both = [obuf[core * 16 + g * 2 + n] for core in range(2) for n in range(2)]
        total = jnp.dot(pick[...], jnp.concatenate(both, axis=0), preferred_element_type=F32)
        proj[g * TILES * 16 : (g + 1) * TILES * 16, :] = total
        for j in range(TILES):
            val = total[j * 16 : (j + 1) * 16]
            square = square + val * val
    mean = jnp.sum(square, axis=1, keepdims=True) / (8 * WIDE)
    factor = lax.rsqrt(mean + 1e-6)
    for n in range(8 * TILES):
        cols = slice(n * HD, (n + 1) * HD)
        val = proj[n * 16 : (n + 1) * 16, :] * factor * gainv[n : n + 1, :]
        out_ref[:, cols] = (resv[:, cols].astype(F32) + val).astype(BF)


def per_device(queries, keys, values, out_weight, residual, norm_gain, lengths, owner_blocks):
    nt = lax.axis_size("tp")
    docs = lengths.shape[0]
    width = out_weight.shape[1]
    orows = residual.shape[0]
    any_spec = pl.BlockSpec(memory_space=pl.ANY)
    vmem = pltpu.VMEM
    dma = pltpu.SemaphoreType.DMA
    scratch = dict(
        qbuf=vmem((2, TOK, HD), BF),
        vtmp=vmem((TOK, HD), BF),
        kv=vmem((2, CHIPS, 2, TOK, HD), BF),
        qt=vmem((HD, CT), BF),
        acc=vmem((HD, CT), F32),
        stat=vmem((8, CT), F32),
        send1=vmem((CT, HD), BF),
        recv1=vmem((CT, HD), BF),
        perm=vmem((CT, CT), BF),
        perm2=vmem((CT, CT), BF),
        send2=vmem((CT, HD), BF),
        abuf=vmem((2, SIDE, nt, 32, HD), BF),
        wbuf=vmem((nt, 2, 64, WIDE), BF),
        part=vmem((2 * WIDE + 256, HD), F32),
        osend=vmem((PLANE, 48, HD), BF),
        obuf=vmem((PLANE, 48, HD), BF),
        pick=vmem((TILES * 16, 192), BF),
        proj=vmem((8 * TILES * 16, HD), F32),
        resv=vmem((orows, width), BF),
        gainv=vmem((width // HD, HD), F32),
        hail_sem=pltpu.SemaphoreType.REGULAR((3,)),
        loc_sem=dma((6,)),
        q_sem=dma((2,)),
        kv_send=dma((9,)),
        fwd_send=dma((2, 3)),
        kv_recv=dma((9,)),
        sib_send=dma((CHIPS,)),
        sib_recv=dma((CHIPS,)),
        w_send=dma((2, 8)),
        w_recv=dma((2, 8)),
        wv_send=dma((16,)),
        wv_recv=dma((16,)),
        a1_send=dma((CHIPS,)),
        a1_recv=dma((CHIPS,)),
        z_send=dma((16,)),
        z_recv=dma((16,)),
        ag_send=dma((2, 2, SIDE)),
        ag_recv=dma((2, SIDE, 2)),
        fin_send=dma((PLANE,)),
        fin_recv=dma((PLANE,)),
    )
    return pl.pallas_call(
        functools.partial(kernel, nt, docs),
        out_shape=jax.ShapeDtypeStruct((orows, width), BF),
        in_specs=[any_spec] * 6
        + [pl.BlockSpec(memory_space=pltpu.SMEM)] * 2,
        out_specs=pl.BlockSpec(memory_space=pltpu.VMEM),
        scratch_shapes=list(scratch.values()),
        compiler_params=pltpu.CompilerParams(
            collective_id=0, has_side_effects=True, vmem_limit_bytes=60 * 1024 * 1024
        ),
        name="attend_project",
    )(
        queries,
        keys,
        values,
        out_weight,
        residual,
        norm_gain.reshape(width // HD, HD),
        lengths,
        owner_blocks.T,
    )


def solution(mesh):
    in_specs = (
        P("ctx", "tp"),
        P("ctx", "tp"),
        P("ctx", "tp"),
        P("tp", None),
        P(("ctx", "tp"), None),
        P(),
        P(),
        P(),
    )
    out_specs = P(("ctx", "tp"), None)
    return jax.shard_map(
        per_device, mesh=mesh, in_specs=in_specs, out_specs=out_specs, check_vma=False
    )
```

```python
import functools
import math

import jax
import jax.numpy as jnp
from jax import lax
from jax.experimental import pallas as pl
from jax.experimental.pallas import tpu as pltpu
from jax.sharding import PartitionSpec as P

MESH = pl.DeviceIdType.MESH

HD = 128
BLOCK = 128
TOK = 256
SIDE = 4
CHIPS = SIDE * SIDE
CT = 2 * TOK
PLANE = 2 * CHIPS
TILES = 5
WIDE = TILES * HD
FLOOR = -1e30
SCALE = math.log2(math.e) / math.sqrt(HD)
BF = jnp.bfloat16
F32 = jnp.float32


def iota(shape, dim):
    return lax.broadcasted_iota(jnp.int32, shape, dim)


def kernel(
    nt,
    docs,
    q_hbm,
    k_hbm,
    v_hbm,
    w_hbm,
    res_hbm,
    gain_hbm,
    len_ref,
    own_ref,
    out_ref,
    qbuf,
    vtmp,
    kv,
    qt,
    acc,
    stat,
    send1,
    recv1,
    perm,
    perm2,
    send2,
    abuf,
    wbuf,
    part,
    osend,
    obuf,
    pick,
    proj,
    resv,
    gainv,
    hail_sem,
    loc_sem,
    q_sem,
    kv_send,
    fwd_send,
    kv_recv,
    sib_send,
    sib_recv,
    w_send,
    w_recv,
    wv_send,
    wv_recv,
    a1_send,
    a1_recv,
    z_send,
    z_recv,
    ag_send,
    ag_recv,
    fin_send,
    fin_recv,
):
    orows = out_ref.shape[0]
    me = lax.axis_index("ctx")
    t = lax.axis_index("tp")
    c = me // 2
    h = me % 2
    sib = (me + 1 - 2 * h, t)
    x = c % SIDE
    y = c // SIDE
    u = x + h * (y - x)
    v = y + h * (x - y)

    def chip(uu, vv):
        return (uu % SIDE) * (1 + 3 * h) + (vv % SIDE) * (4 - 3 * h)

    def remote(src, dst, ssem, rsem, dev):
        return pltpu.make_async_remote_copy(
            src_ref=src, dst_ref=dst, send_sem=ssem, recv_sem=rsem, device_id=dev, device_id_type=MESH
        )

    head = pl.multiple_of(h * HD, HD)
    other_head = pl.multiple_of((1 - h) * HD, HD)
    HERE = nt // 4
    low, high = v % 2, v // 2
    w_rows = pl.ds(pl.multiple_of(h * HD + low * 64, 64), 64)
    w_cols = pl.ds(pl.multiple_of((u * 2 + high) * WIDE, HD), WIDE)
    loads = [
        (k_hbm, kv.at[h, c, 0]),
        (v_hbm, vtmp),
        (q_hbm.at[:, pl.ds(head, HD)], qbuf.at[h]),
        (w_hbm.at[w_rows, w_cols], wbuf.at[HERE, low]),
        (res_hbm, resv),
        (gain_hbm, gainv),
    ]
    loads = [pltpu.make_async_copy(s, d, loc_sem.at[n]) for n, (s, d) in enumerate(loads)]
    for copy in loads:
        copy.start()
    barrier = pltpu.get_barrier_semaphore()

    @pl.loop(1, CHIPS)
    def _(d):
        pl.semaphore_signal(barrier, inc=1, device_id=((me + 2 * d) % PLANE, t), device_id_type=MESH)

    right = (me, (t + 1) % nt)
    left = (me, (t + nt - 1) % nt)
    for dev in (right, left, sib):
        pl.semaphore_signal(barrier, inc=1, device_id=dev, device_id_type=MESH)

    row = iota((CT, 1), 0)
    target = (row % 16) * 32 + (row // BLOCK) * 8 + (row % BLOCK) // 16
    spread = jnp.where(iota((CT, CT), 1) == target, 1.0, 0.0).astype(BF)
    perm[...] = spread
    lane = iota((1, CT), 1)
    pos = c * CT + ((lane // 8) % 4) * BLOCK + (lane % 8) * 16 + lane // 32
    first = jnp.zeros((1, CT), jnp.int32)
    end = jnp.int32(0)
    for n in range(docs):
        end = end + len_ref[n]
        first = jnp.where(end <= pos, end, first)

    for k in range(2):
        owned = jnp.zeros((PLANE, 1), jnp.int32)
        for o in range(PLANE):
            owned = jnp.where(iota((PLANE, 1), 0) == o, own_ref[k, o] * 8, owned)
        for i in range(8):
            rows = slice((k * 8 + i) * PLANE, (k * 8 + i + 1) * PLANE)
            perm2[rows, :] = jnp.where(iota((PLANE, CT), 1) == owned + i, 1.0, 0.0).astype(BF)

    row = iota((TILES * 16, 1), 0)
    tile_of = row // 16
    chip_of = row % 16
    lane = iota((TILES * 16, 192), 1)

    def place(uu, vv):
        return (vv % 2) * 48 + tile_of * 8 + (vv // 2) * 4 + uu

    picked = (lane == place(chip_of % 4, chip_of // 4)) | (lane == 96 + place(chip_of // 4, chip_of % 4))
    pick[...] = jnp.where(picked, 1.0, 0.0).astype(BF)
    part[2 * WIDE :, :] = jnp.zeros((256, HD), F32)

    loads[0].wait()
    loads[1].wait()
    vt = vtmp[...].astype(F32)
    for n in range(TOK // HD):
        kv[h, c, 1, n * HD : (n + 1) * HD, :] = vt[n * HD : (n + 1) * HD, :].T.astype(BF)
    loads[2].wait()
    loads[3].wait()

    pl.semaphore_wait(barrier, CHIPS + 2)

    def hail(n):
        for dev in ((me, (t + 2**n) % nt), (me, (t + nt - 2**n) % nt)):
            pl.semaphore_signal(hail_sem.at[n], inc=1, device_id=dev, device_id_type=MESH)

    def heard(n):
        pl.semaphore_wait(hail_sem.at[n], 2)

    hail(0)

    rsteps = nt // 2
    lsteps = nt - 1 - rsteps

    def w_copy(way, step):
        sign = 1 if way else -1
        src = wbuf.at[(HERE + sign * step) % nt, low]
        dst = wbuf.at[(HERE + sign * (step + 1)) % nt, low]
        return remote(src, dst, w_send.at[way, step], w_recv.at[way, step], left if way else right)

    def w_spread(slot):
        ref = wbuf.at[slot, low]
        return remote(ref, ref, wv_send.at[slot], wv_recv.at[slot], (chip(u, v + 1 - 2 * low) * 2 + h, t))

    def w_step(step):
        for way, count in ((0, rsteps), (1, lsteps)):
            if step >= 1 and step - 1 < count:
                w_copy(way, step - 1).wait_recv()
            if step < count:
                w_copy(way, step).start()

    def w_share(step):
        for way, count in ((0, rsteps), (1, lsteps)):
            if (step >= 1 and step - 1 < count) or (step == 0 and way == 0):
                w_spread((HERE + (1 if way else -1) * step) % nt).start()

    def w_finish():
        for way, count in ((0, rsteps), (1, lsteps)):
            for step in range(count):
                w_copy(way, step).wait_send()
        for slot in range(nt):
            w_spread(slot).wait_send()

    def w_arrived(slots):
        for slot in slots:
            ref = wbuf.at[slot, 1 - low]
            remote(ref, ref, wv_send.at[slot], wv_recv.at[slot], sib).wait_recv()

    def attend(src, start):
        keys = jnp.concatenate([kv[0, src, 0], kv[1, src, 0]], axis=0)
        pieces = []
        for core in range(2):
            block = kv[core, src, 1]
            pieces += [block[n * HD : (n + 1) * HD] for n in range(TOK // HD)]
        values = jnp.concatenate(pieces, axis=1)
        wide = 256
        for n in range(CT // wide):
            cols = slice(n * wide, (n + 1) * wide)
            score = jnp.dot(keys, qt[:, cols], preferred_element_type=F32) * SCALE
            kpos = src * CT + iota((CT, wide), 0)
            visible = kpos >= first[:, cols]
            if start:
                visible = visible & (kpos <= pos[:, cols])
            score = jnp.where(visible, score, FLOOR)
            top = jnp.max(score, axis=0, keepdims=True)
            if not start:
                old = stat[0:1, cols]
                top = jnp.maximum(top, old)
                decay = jnp.exp2(old - top)
            weight = jnp.exp2(score - top)
            total = jnp.sum(weight, axis=0, keepdims=True)
            context = jnp.dot(values, weight.astype(BF), preferred_element_type=F32)
            if not start:
                total = total + stat[1:2, cols] * decay
                context = context + acc[:, cols] * decay
            stat[0:1, cols] = top
            stat[1:2, cols] = total
            acc[:, cols] = context

    def swap_copy(src):
        ref = kv.at[h, src]
        return remote(ref, ref, sib_send.at[src], sib_recv.at[src], sib)

    def swap_wait(src):
        ref = kv.at[1 - h, src]
        remote(ref, ref, sib_send.at[src], sib_recv.at[src], sib).wait_recv()

    q_send = remote(q_hbm.at[:, pl.ds(other_head, HD)], qbuf.at[h], q_sem.at[0], q_sem.at[1], sib)
    q_send.start()

    def kv_copy(src, ssem, to):
        ref = kv.at[h, src]
        return remote(ref, ref, ssem, kv_recv.at[to - src], (to * 2 + h, t))

    own_sends = [(4, y < 3), (8, y < 2), (1, x < 3), (2, x < 2), (3, x < 1)]

    def forwards(dy):
        for dx in range(1, SIDE):
            to = y * SIDE + (x + dx) % SIDE
            yield kv_copy(c - 4 * dy, fwd_send.at[dy - 1, dx - 1], to), (y >= dy) & ((dy == 1) | (x + dx >= SIDE))

    for k, cond in own_sends:

        @pl.when(cond)
        def _():
            kv_copy(c, kv_send.at[k], c + k).start()

    swap_copy(c).start()
    w_step(0)
    q_send.wait_recv()
    for core in range(2):
        rows = qbuf[core].astype(F32).T.astype(BF)
        some = jnp.dot(rows, perm[core * TOK : (core + 1) * TOK, :], preferred_element_type=F32)
        if core == 0:
            total = some
        else:
            total = total + some
    qt[...] = total.astype(BF)
    heard(0)
    hail(1)
    swap_wait(c)
    attend(c, True)

    w_step(1)

    for dy in (1, 2):

        @pl.when(y >= dy)
        def _():
            kv_copy(c - 4 * dy, kv_send.at[0], c).wait_recv()

        for copy, cond in forwards(dy):

            @pl.when(cond)
            def _():
                copy.start()

    w_share(0)
    w_share(1)
    heard(1)
    hail(2)

    def back(i):
        return jnp.where(i == 1, 4, jnp.where(i == 2, 8, jnp.where(i < 6, i - 2, i - 1)))

    @pl.loop(1, 10)
    def _(i):
        k = back(i)

        @pl.when((i < 9) & (k <= c))
        def _():
            @pl.when(i > 2)
            def _():
                kv_copy(c - k, kv_send.at[0], c).wait_recv()

            swap_copy(c - k).start()

        for step, at in ((2, 5), (3, 8)):

            @pl.when(i == at)
            def _():
                w_step(step)
                w_share(step)

        before = back(i - 1)

        @pl.when((i >= 2) & (before <= c))
        def _():
            swap_wait(c - before)
            attend(c - before, False)

    result = (acc[...] / stat[1:2, :]).T.astype(BF)
    send1[...] = result

    def a1_copy(d):
        to = (c + d) % CHIPS
        return remote(
            send1.at[pl.ds(pl.multiple_of(to * 32, 32), 32)],
            recv1.at[pl.ds(pl.multiple_of(c * 32, 32), 32)],
            a1_send.at[d],
            a1_recv.at[d],
            (to * 2 + h, t),
        )

    def outward(n, size):
        return (size // 2 + (n + 1) // 2 * (1 - 2 * (n % 2))) % size

    @pl.loop(0, CHIPS - 1)
    def _(n):
        a1_copy(outward(n, CHIPS)).start()

    w_step(4)
    w_share(4)
    w_step(5)
    w_share(5)
    mine = pl.ds(pl.multiple_of(c * 32, 32), 32)
    recv1[mine, :] = send1[mine, :]

    @pl.loop(1, CHIPS)
    def _(d):
        a1_copy(d).wait()


    send2[...] = jnp.dot(perm2[...], recv1[...], preferred_element_type=F32).astype(BF)

    heard(2)

    def z_copy(d):
        to = (t + d) % nt
        return remote(
            send2.at[pl.ds(pl.multiple_of(to * 32, 32), 32)],
            abuf.at[high, u, (HERE - d + nt) % nt],
            z_send.at[d],
            z_recv.at[d],
            (me, to),
        )

    @pl.loop(0, nt - 1)
    def _(n):
        z_copy(outward(n, nt)).start()

    abuf[high, u, HERE] = send2[pl.ds(pl.multiple_of(t * 32, 32), 32), :]
    w_step(6)
    w_share(6)

    lower = nt // 2

    def ag_copy(own, du, side):
        at = high if own == 0 else 1 - high
        ref = abuf.at[at, u, pl.ds(side * lower, lower)]
        to = chip(u, v + 2) if du == 0 else chip(u + du, v)
        return remote(ref, ref, ag_send.at[own, side, du], ag_recv.at[at, u, side], (to * 2 + h, t))

    def ag_arrived(own, du, side):
        at = high if own == 0 else 1 - high
        uu = (u + du) % SIDE
        ref = abuf.at[at, uu, pl.ds(side * lower, lower)]
        remote(ref, ref, ag_send.at[0, 0, 0], ag_recv.at[at, uu, side], sib).wait_recv()

    def ag_all(side):
        for own in (0, 1):
            for du in (1, 3, 2):
                ag_arrived(own, du, side)

    def ag_onward(side):
        ag_arrived(1, 0, side)
        for du in (2, 1, 3):
            ag_copy(1, du, side).start()

    def product(side):
        lhs = [abuf[:, :, side * lower + n].reshape(2 * SIDE * 32, HD) for n in range(lower)]
        lhs = jnp.concatenate(lhs, axis=1)
        for first_tile in range(0, TILES, 2):
            tiles = min(2, TILES - first_tile)
            rhs = wbuf[side * lower : (side + 1) * lower, :, :, first_tile * HD : (first_tile + tiles) * HD]
            val = jnp.dot(lhs, rhs.reshape(lower * HD, tiles * HD), preferred_element_type=F32)
            for m in range(tiles):
                rows = slice((first_tile + m) * 256, (first_tile + m + 1) * 256)
                piece = val[:, m * HD : (m + 1) * HD]
                part[rows, :] = piece if side == 0 else part[rows, :] + piece

    @pl.loop(1, nt)
    def _(d):
        @pl.when((d <= HERE) | (d > nt - HERE))
        def _():
            z_copy(d).wait()

    for du in (0, 2, 1, 3):
        ag_copy(0, du, 0).start()
    w_step(7)
    w_share(7)

    @pl.loop(1, nt)
    def _(d):
        @pl.when((d > HERE) & (d <= nt - HERE))
        def _():
            z_copy(d).wait()

    for du in (0, 2, 1, 3):
        ag_copy(0, du, 1).start()
    ag_onward(0)
    w_step(8)
    w_share(8)
    ag_onward(1)
    ag_all(0)
    w_arrived(range(lower))
    product(0)
    ag_all(1)
    w_arrived(range(lower, nt))
    product(1)

    for o in range(PLANE):
        osend[o] = part[pl.ds(o, 48, stride=32), :].astype(BF)

    mine = (h * SIDE + u) * SIDE + v

    def fin_copy(d):
        to = (me + d) % PLANE
        return remote(osend.at[to], obuf.at[mine], fin_send.at[d], fin_recv.at[d], (to, t))

    @pl.loop(1, PLANE)
    def _(d):
        fin_copy(outward(d - 1, PLANE)).start()

    obuf[mine] = osend[me]
    loads[4].wait()
    loads[5].wait()
    w_finish()
    for own, du in ((0, 0), (0, 1), (0, 2), (0, 3), (1, 1), (1, 2), (1, 3)):
        for side in range(2):
            ag_copy(own, du, side).wait_send()

    q_send.wait_send()

    @pl.loop(0, jnp.minimum(c, 8) + 1)
    def _(k):
        swap_copy(c - k).wait_send()

    for k, cond in own_sends:

        @pl.when(cond)
        def _():
            kv_copy(c, kv_send.at[k], c + k).wait_send()

    for dy in (1, 2):
        for copy, cond in forwards(dy):

            @pl.when(cond)
            def _():
                copy.wait_send()

    @pl.loop(1, PLANE)
    def _(d):
        fin_copy(d).wait()

    square = jnp.zeros((orows, HD), F32)
    for g in range(2 * SIDE):
        both = [obuf[core * 16 + g * 2 + n] for core in range(2) for n in range(2)]
        total = jnp.dot(pick[...], jnp.concatenate(both, axis=0), preferred_element_type=F32)
        proj[g * TILES * 16 : (g + 1) * TILES * 16, :] = total
        for j in range(TILES):
            val = total[j * 16 : (j + 1) * 16]
            square = square + val * val
    mean = jnp.sum(square, axis=1, keepdims=True) / (8 * WIDE)
    factor = lax.rsqrt(mean + 1e-6)
    for n in range(8 * TILES):
        cols = slice(n * HD, (n + 1) * HD)
        val = proj[n * 16 : (n + 1) * 16, :] * factor * gainv[n : n + 1, :]
        out_ref[:, cols] = (resv[:, cols].astype(F32) + val).astype(BF)


def per_device(queries, keys, values, out_weight, residual, norm_gain, lengths, owner_blocks):
    nt = lax.axis_size("tp")
    docs = lengths.shape[0]
    width = out_weight.shape[1]
    orows = residual.shape[0]
    any_spec = pl.BlockSpec(memory_space=pl.ANY)
    vmem = pltpu.VMEM
    dma = pltpu.SemaphoreType.DMA
    scratch = dict(
        qbuf=vmem((2, TOK, HD), BF),
        vtmp=vmem((TOK, HD), BF),
        kv=vmem((2, CHIPS, 2, TOK, HD), BF),
        qt=vmem((HD, CT), BF),
        acc=vmem((HD, CT), F32),
        stat=vmem((8, CT), F32),
        send1=vmem((CT, HD), BF),
        recv1=vmem((CT, HD), BF),
        perm=vmem((CT, CT), BF),
        perm2=vmem((CT, CT), BF),
        send2=vmem((CT, HD), BF),
        abuf=vmem((2, SIDE, nt, 32, HD), BF),
        wbuf=vmem((nt, 2, 64, WIDE), BF),
        part=vmem((2 * WIDE + 256, HD), F32),
        osend=vmem((PLANE, 48, HD), BF),
        obuf=vmem((PLANE, 48, HD), BF),
        pick=vmem((TILES * 16, 192), BF),
        proj=vmem((8 * TILES * 16, HD), F32),
        resv=vmem((orows, width), BF),
        gainv=vmem((width // HD, HD), F32),
        hail_sem=pltpu.SemaphoreType.REGULAR((3,)),
        loc_sem=dma((6,)),
        q_sem=dma((2,)),
        kv_send=dma((9,)),
        fwd_send=dma((2, 3)),
        kv_recv=dma((9,)),
        sib_send=dma((CHIPS,)),
        sib_recv=dma((CHIPS,)),
        w_send=dma((2, 8)),
        w_recv=dma((2, 8)),
        wv_send=dma((16,)),
        wv_recv=dma((16,)),
        a1_send=dma((CHIPS,)),
        a1_recv=dma((CHIPS,)),
        z_send=dma((16,)),
        z_recv=dma((16,)),
        ag_send=dma((2, 2, SIDE)),
        ag_recv=dma((2, SIDE, 2)),
        fin_send=dma((PLANE,)),
        fin_recv=dma((PLANE,)),
    )
    return pl.pallas_call(
        functools.partial(kernel, nt, docs),
        out_shape=jax.ShapeDtypeStruct((orows, width), BF),
        in_specs=[any_spec] * 6
        + [pl.BlockSpec(memory_space=pltpu.SMEM)] * 2,
        out_specs=pl.BlockSpec(memory_space=pltpu.VMEM),
        scratch_shapes=list(scratch.values()),
        compiler_params=pltpu.CompilerParams(
            collective_id=0, has_side_effects=True, vmem_limit_bytes=60 * 1024 * 1024
        ),
        name="attend_project",
    )(
        queries,
        keys,
        values,
        out_weight,
        residual,
        norm_gain.reshape(width // HD, HD),
        lengths,
        owner_blocks.T,
    )


def solution(mesh):
    in_specs = (
        P("ctx", "tp"),
        P("ctx", "tp"),
        P("ctx", "tp"),
        P("tp", None),
        P(("ctx", "tp"), None),
        P(),
        P(),
        P(),
    )
    out_specs = P(("ctx", "tp"), None)
    return jax.shard_map(
        per_device, mesh=mesh, in_specs=in_specs, out_specs=out_specs, check_vma=False
    )
```

```python
import functools
import math

import jax
import jax.numpy as jnp
from jax import lax
from jax.experimental import pallas as pl
from jax.experimental.pallas import tpu as pltpu
from jax.sharding import PartitionSpec as P

MESH = pl.DeviceIdType.MESH

HD = 128
BLOCK = 128
TOK = 256
SIDE = 4
CHIPS = SIDE * SIDE
CT = 2 * TOK
PLANE = 2 * CHIPS
TILES = 5
WIDE = TILES * HD
FLOOR = -1e30
SCALE = math.log2(math.e) / math.sqrt(HD)
BF = jnp.bfloat16
F32 = jnp.float32


def iota(shape, dim):
    return lax.broadcasted_iota(jnp.int32, shape, dim)


def kernel(
    nt,
    docs,
    q_hbm,
    k_hbm,
    v_hbm,
    w_hbm,
    res_hbm,
    gain_hbm,
    len_hbm,
    own_hbm,
    out_ref,
    len_ref,
    own_ref,
    qbuf,
    vtmp,
    kv,
    qt,
    acc,
    stat,
    send1,
    recv1,
    perm,
    perm2,
    send2,
    abuf,
    wbuf,
    part,
    osend,
    obuf,
    pick,
    proj,
    resv,
    gainv,
    hail_sem,
    loc_sem,
    q_sem,
    kv_send,
    fwd_send,
    kv_recv,
    sib_send,
    sib_recv,
    w_send,
    w_recv,
    wv_send,
    wv_recv,
    a1_send,
    a1_recv,
    z_send,
    z_recv,
    ag_send,
    ag_recv,
    fin_send,
    fin_recv,
):
    orows = out_ref.shape[0]
    me = lax.axis_index("ctx")
    t = lax.axis_index("tp")
    c = me // 2
    h = me % 2
    sib = (me + 1 - 2 * h, t)
    x = c % SIDE
    y = c // SIDE
    u = x + h * (y - x)
    v = y + h * (x - y)

    def chip(uu, vv):
        return (uu % SIDE) * (1 + 3 * h) + (vv % SIDE) * (4 - 3 * h)

    def remote(src, dst, ssem, rsem, dev):
        return pltpu.make_async_remote_copy(
            src_ref=src, dst_ref=dst, send_sem=ssem, recv_sem=rsem, device_id=dev, device_id_type=MESH
        )

    head = pl.multiple_of(h * HD, HD)
    other_head = pl.multiple_of((1 - h) * HD, HD)
    HERE = nt // 4
    low, high = v % 2, v // 2
    w_rows = pl.ds(pl.multiple_of(h * HD + low * 64, 64), 64)
    w_cols = pl.ds(pl.multiple_of((u * 2 + high) * WIDE, HD), WIDE)
    loads = [
        (k_hbm, kv.at[h, c, 0]),
        (v_hbm, vtmp),
        (q_hbm.at[:, pl.ds(head, HD)], qbuf.at[h]),
        (w_hbm.at[w_rows, w_cols], wbuf.at[HERE, low]),
        (res_hbm, resv),
        (gain_hbm, gainv),
        (len_hbm, len_ref),
        (own_hbm, own_ref),
    ]
    loads = [pltpu.make_async_copy(s, d, loc_sem.at[n]) for n, (s, d) in enumerate(loads)]
    for copy in loads:
        copy.start()
    barrier = pltpu.get_barrier_semaphore()

    @pl.loop(1, CHIPS)
    def _(d):
        pl.semaphore_signal(barrier, inc=1, device_id=((me + 2 * d) % PLANE, t), device_id_type=MESH)

    right = (me, (t + 1) % nt)
    left = (me, (t + nt - 1) % nt)
    for dev in (right, left, sib):
        pl.semaphore_signal(barrier, inc=1, device_id=dev, device_id_type=MESH)

    row = iota((CT, 1), 0)
    target = (row % 16) * 32 + (row // BLOCK) * 8 + (row % BLOCK) // 16
    spread = jnp.where(iota((CT, CT), 1) == target, 1.0, 0.0).astype(BF)
    perm[...] = spread
    lane = iota((1, CT), 1)
    pos = c * CT + ((lane // 8) % 4) * BLOCK + (lane % 8) * 16 + lane // 32
    first = jnp.zeros((1, CT), jnp.int32)
    end = jnp.int32(0)
    loads[6].wait()
    loads[7].wait()
    for n in range(docs):
        end = end + len_ref[n]
        first = jnp.where(end <= pos, end, first)

    for k in range(2):
        owned = jnp.zeros((PLANE, 1), jnp.int32)
        for o in range(PLANE):
            owned = jnp.where(iota((PLANE, 1), 0) == o, own_ref[k, o] * 8, owned)
        for i in range(8):
            rows = slice((k * 8 + i) * PLANE, (k * 8 + i + 1) * PLANE)
            perm2[rows, :] = jnp.where(iota((PLANE, CT), 1) == owned + i, 1.0, 0.0).astype(BF)

    row = iota((TILES * 16, 1), 0)
    tile_of = row // 16
    chip_of = row % 16
    lane = iota((TILES * 16, 192), 1)

    def place(uu, vv):
        return (vv % 2) * 48 + tile_of * 8 + (vv // 2) * 4 + uu

    picked = (lane == place(chip_of % 4, chip_of // 4)) | (lane == 96 + place(chip_of // 4, chip_of % 4))
    pick[...] = jnp.where(picked, 1.0, 0.0).astype(BF)
    part[2 * WIDE :, :] = jnp.zeros((256, HD), F32)

    loads[0].wait()
    loads[1].wait()
    vt = vtmp[...].astype(F32)
    for n in range(TOK // HD):
        kv[h, c, 1, n * HD : (n + 1) * HD, :] = vt[n * HD : (n + 1) * HD, :].T.astype(BF)
    loads[2].wait()
    loads[3].wait()

    pl.semaphore_wait(barrier, CHIPS + 2)

    def hail(n):
        for dev in ((me, (t + 2**n) % nt), (me, (t + nt - 2**n) % nt)):
            pl.semaphore_signal(hail_sem.at[n], inc=1, device_id=dev, device_id_type=MESH)

    def heard(n):
        pl.semaphore_wait(hail_sem.at[n], 2)

    hail(0)

    rsteps = nt // 2
    lsteps = nt - 1 - rsteps

    def w_copy(way, step):
        sign = 1 if way else -1
        src = wbuf.at[(HERE + sign * step) % nt, low]
        dst = wbuf.at[(HERE + sign * (step + 1)) % nt, low]
        return remote(src, dst, w_send.at[way, step], w_recv.at[way, step], left if way else right)

    def w_spread(slot):
        ref = wbuf.at[slot, low]
        return remote(ref, ref, wv_send.at[slot], wv_recv.at[slot], (chip(u, v + 1 - 2 * low) * 2 + h, t))

    def w_step(step):
        for way, count in ((0, rsteps), (1, lsteps)):
            if step >= 1 and step - 1 < count:
                w_copy(way, step - 1).wait_recv()
            if step < count:
                w_copy(way, step).start()

    def w_share(step):
        for way, count in ((0, rsteps), (1, lsteps)):
            if (step >= 1 and step - 1 < count) or (step == 0 and way == 0):
                w_spread((HERE + (1 if way else -1) * step) % nt).start()

    def w_finish():
        for way, count in ((0, rsteps), (1, lsteps)):
            for step in range(count):
                w_copy(way, step).wait_send()
        for slot in range(nt):
            w_spread(slot).wait_send()

    def w_arrived(slots):
        for slot in slots:
            ref = wbuf.at[slot, 1 - low]
            remote(ref, ref, wv_send.at[slot], wv_recv.at[slot], sib).wait_recv()

    def attend(src, start):
        keys = jnp.concatenate([kv[0, src, 0], kv[1, src, 0]], axis=0)
        pieces = []
        for core in range(2):
            block = kv[core, src, 1]
            pieces += [block[n * HD : (n + 1) * HD] for n in range(TOK // HD)]
        values = jnp.concatenate(pieces, axis=1)
        wide = 256
        for n in range(CT // wide):
            cols = slice(n * wide, (n + 1) * wide)
            score = jnp.dot(keys, qt[:, cols], preferred_element_type=F32) * SCALE
            kpos = src * CT + iota((CT, wide), 0)
            visible = kpos >= first[:, cols]
            if start:
                visible = visible & (kpos <= pos[:, cols])
            score = jnp.where(visible, score, FLOOR)
            top = jnp.max(score, axis=0, keepdims=True)
            if not start:
                old = stat[0:1, cols]
                top = jnp.maximum(top, old)
                decay = jnp.exp2(old - top)
            weight = jnp.exp2(score - top)
            total = jnp.sum(weight, axis=0, keepdims=True)
            context = jnp.dot(values, weight.astype(BF), preferred_element_type=F32)
            if not start:
                total = total + stat[1:2, cols] * decay
                context = context + acc[:, cols] * decay
            stat[0:1, cols] = top
            stat[1:2, cols] = total
            acc[:, cols] = context

    def swap_copy(src):
        ref = kv.at[h, src]
        return remote(ref, ref, sib_send.at[src], sib_recv.at[src], sib)

    def swap_wait(src):
        ref = kv.at[1 - h, src]
        remote(ref, ref, sib_send.at[src], sib_recv.at[src], sib).wait_recv()

    q_send = remote(q_hbm.at[:, pl.ds(other_head, HD)], qbuf.at[h], q_sem.at[0], q_sem.at[1], sib)
    q_send.start()

    def kv_copy(src, ssem, to, part):
        ref = kv.at[h, src, part]
        return remote(ref, ref, ssem, kv_recv.at[to - src, part], (to * 2 + h, t))

    own_sends = [(4, y < 3), (8, y < 2), (1, x < 3), (2, x < 2), (3, x < 1)]

    def forwards(dy, part):
        for dx in range(1, SIDE):
            to = y * SIDE + (x + dx) % SIDE
            yield kv_copy(c - 4 * dy, fwd_send.at[dy - 1, dx - 1, part], to, part), (y >= dy) & ((dy == 1) | (x + dx >= SIDE))

    for k, cond in own_sends:

        @pl.when(cond)
        def _():
            for side in range(2):
                kv_copy(c, kv_send.at[k, side], c + k, side).start()

    swap_copy(c).start()
    w_step(0)
    q_send.wait_recv()
    for core in range(2):
        rows = qbuf[core].astype(F32).T.astype(BF)
        some = jnp.dot(rows, perm[core * TOK : (core + 1) * TOK, :], preferred_element_type=F32)
        if core == 0:
            total = some
        else:
            total = total + some
    qt[...] = total.astype(BF)
    heard(0)
    hail(1)
    swap_wait(c)
    attend(c, True)

    w_step(1)

    for dy, side in ((1, 0), (1, 1), (2, 0), (2, 1)):

        @pl.when(y >= dy)
        def _():
            kv_copy(c - 4 * dy, kv_send.at[0, 0], c, side).wait_recv()

        for copy, cond in forwards(dy, side):

            @pl.when(cond)
            def _():
                copy.start()

    w_share(0)
    w_share(1)
    heard(1)
    hail(2)

    def back(i):
        return jnp.where(i == 1, 4, jnp.where(i == 2, 8, jnp.where(i < 6, i - 2, i - 1)))

    @pl.loop(1, 10)
    def _(i):
        k = back(i)

        @pl.when((i < 9) & (k <= c))
        def _():
            @pl.when(i > 2)
            def _():
                for side in range(2):
                    kv_copy(c - k, kv_send.at[0, 0], c, side).wait_recv()

            swap_copy(c - k).start()

        for step, at in ((2, 5), (3, 8)):

            @pl.when(i == at)
            def _():
                w_step(step)
                w_share(step)

        before = back(i - 1)

        @pl.when((i >= 2) & (before <= c))
        def _():
            swap_wait(c - before)
            attend(c - before, False)

    result = (acc[...] / stat[1:2, :]).T.astype(BF)
    send1[...] = result

    def a1_copy(d):
        to = (c + d) % CHIPS
        return remote(
            send1.at[pl.ds(pl.multiple_of(to * 32, 32), 32)],
            recv1.at[pl.ds(pl.multiple_of(c * 32, 32), 32)],
            a1_send.at[d],
            a1_recv.at[d],
            (to * 2 + h, t),
        )

    def outward(n, size):
        return (size // 2 + (n + 1) // 2 * (1 - 2 * (n % 2))) % size

    @pl.loop(0, CHIPS - 1)
    def _(n):
        a1_copy(outward(n, CHIPS)).start()

    w_step(4)
    w_share(4)
    w_step(5)
    w_share(5)
    mine = pl.ds(pl.multiple_of(c * 32, 32), 32)
    recv1[mine, :] = send1[mine, :]

    @pl.loop(1, CHIPS)
    def _(d):
        a1_copy(d).wait()


    send2[...] = jnp.dot(perm2[...], recv1[...], preferred_element_type=F32).astype(BF)

    heard(2)

    def z_copy(d):
        to = (t + d) % nt
        return remote(
            send2.at[pl.ds(pl.multiple_of(to * 32, 32), 32)],
            abuf.at[high, u, (HERE - d + nt) % nt],
            z_send.at[d],
            z_recv.at[d],
            (me, to),
        )

    @pl.loop(0, nt - 1)
    def _(n):
        z_copy(outward(n, nt)).start()

    abuf[high, u, HERE] = send2[pl.ds(pl.multiple_of(t * 32, 32), 32), :]
    w_step(6)
    w_share(6)

    lower = nt // 2

    def ag_copy(own, du, side):
        at = high if own == 0 else 1 - high
        ref = abuf.at[at, u, pl.ds(side * lower, lower)]
        to = chip(u, v + 2) if du == 0 else chip(u + du, v)
        return remote(ref, ref, ag_send.at[own, side, du], ag_recv.at[at, u, side], (to * 2 + h, t))

    def ag_arrived(own, du, side):
        at = high if own == 0 else 1 - high
        uu = (u + du) % SIDE
        ref = abuf.at[at, uu, pl.ds(side * lower, lower)]
        remote(ref, ref, ag_send.at[0, 0, 0], ag_recv.at[at, uu, side], sib).wait_recv()

    def ag_all(side):
        for own in (0, 1):
            for du in (1, 3, 2):
                ag_arrived(own, du, side)

    def ag_onward(side):
        ag_arrived(1, 0, side)
        for du in (2, 1, 3):
            ag_copy(1, du, side).start()

    def product(side):
        lhs = [abuf[:, :, side * lower + n].reshape(2 * SIDE * 32, HD) for n in range(lower)]
        lhs = jnp.concatenate(lhs, axis=1)
        for first_tile in range(0, TILES, 2):
            tiles = min(2, TILES - first_tile)
            rhs = wbuf[side * lower : (side + 1) * lower, :, :, first_tile * HD : (first_tile + tiles) * HD]
            val = jnp.dot(lhs, rhs.reshape(lower * HD, tiles * HD), preferred_element_type=F32)
            for m in range(tiles):
                rows = slice((first_tile + m) * 256, (first_tile + m + 1) * 256)
                piece = val[:, m * HD : (m + 1) * HD]
                part[rows, :] = piece if side == 0 else part[rows, :] + piece

    @pl.loop(1, nt)
    def _(d):
        @pl.when((d <= HERE) | (d > nt - HERE))
        def _():
            z_copy(d).wait()

    for du in (0, 2, 1, 3):
        ag_copy(0, du, 0).start()
    w_step(7)
    w_share(7)

    @pl.loop(1, nt)
    def _(d):
        @pl.when((d > HERE) & (d <= nt - HERE))
        def _():
            z_copy(d).wait()

    for du in (0, 2, 1, 3):
        ag_copy(0, du, 1).start()
    ag_onward(0)
    w_step(8)
    w_share(8)
    ag_onward(1)
    ag_all(0)
    w_arrived(range(lower))
    product(0)
    ag_all(1)
    w_arrived(range(lower, nt))
    product(1)

    mine = (h * SIDE + u) * SIDE + v

    def fin_copy(d):
        to = (me + d) % PLANE
        return remote(osend.at[to], obuf.at[mine], fin_send.at[d], fin_recv.at[d], (to, t))

    def pack(o):
        return part[pl.ds(o, 48, stride=32), :].astype(BF)

    @pl.loop(1, PLANE)
    def _(n):
        d = outward(n - 1, PLANE)
        osend[(me + d) % PLANE] = pack((me + d) % PLANE)
        fin_copy(d).start()

    obuf[mine] = pack(me)
    loads[4].wait()
    loads[5].wait()
    w_finish()
    for own, du in ((0, 0), (0, 1), (0, 2), (0, 3), (1, 1), (1, 2), (1, 3)):
        for side in range(2):
            ag_copy(own, du, side).wait_send()

    q_send.wait_send()

    @pl.loop(0, jnp.minimum(c, 8) + 1)
    def _(k):
        swap_copy(c - k).wait_send()

    for k, cond in own_sends:

        @pl.when(cond)
        def _():
            for side in range(2):
                kv_copy(c, kv_send.at[k, side], c + k, side).wait_send()

    for dy, side in ((1, 0), (1, 1), (2, 0), (2, 1)):
        for copy, cond in forwards(dy, side):

            @pl.when(cond)
            def _():
                copy.wait_send()

    @pl.loop(1, PLANE)
    def _(d):
        fin_copy(d).wait()

    square = jnp.zeros((orows, HD), F32)
    for g in range(2 * SIDE):
        both = [obuf[core * 16 + g * 2 + n] for core in range(2) for n in range(2)]
        total = jnp.dot(pick[...], jnp.concatenate(both, axis=0), preferred_element_type=F32)
        proj[g * TILES * 16 : (g + 1) * TILES * 16, :] = total
        for j in range(TILES):
            val = total[j * 16 : (j + 1) * 16]
            square = square + val * val
    mean = jnp.sum(square, axis=1, keepdims=True) / (8 * WIDE)
    factor = lax.rsqrt(mean + 1e-6)
    for n in range(8 * TILES):
        cols = slice(n * HD, (n + 1) * HD)
        val = proj[n * 16 : (n + 1) * 16, :] * factor * gainv[n : n + 1, :]
        out_ref[:, cols] = (resv[:, cols].astype(F32) + val).astype(BF)


def per_device(queries, keys, values, out_weight, residual, norm_gain, lengths, owner_blocks):
    nt = lax.axis_size("tp")
    docs = lengths.shape[0]
    width = out_weight.shape[1]
    orows = residual.shape[0]
    any_spec = pl.BlockSpec(memory_space=pl.ANY)
    vmem = pltpu.VMEM
    dma = pltpu.SemaphoreType.DMA
    scratch = dict(
        len_ref=pltpu.SMEM((docs,), jnp.int32),
        own_ref=pltpu.SMEM((2, PLANE), jnp.int32),
        qbuf=vmem((2, TOK, HD), BF),
        vtmp=vmem((TOK, HD), BF),
        kv=vmem((2, CHIPS, 2, TOK, HD), BF),
        qt=vmem((HD, CT), BF),
        acc=vmem((HD, CT), F32),
        stat=vmem((8, CT), F32),
        send1=vmem((CT, HD), BF),
        recv1=vmem((CT, HD), BF),
        perm=vmem((CT, CT), BF),
        perm2=vmem((CT, CT), BF),
        send2=vmem((CT, HD), BF),
        abuf=vmem((2, SIDE, nt, 32, HD), BF),
        wbuf=vmem((nt, 2, 64, WIDE), BF),
        part=vmem((2 * WIDE + 256, HD), F32),
        osend=vmem((PLANE, 48, HD), BF),
        obuf=vmem((PLANE, 48, HD), BF),
        pick=vmem((TILES * 16, 192), BF),
        proj=vmem((8 * TILES * 16, HD), F32),
        resv=vmem((orows, width), BF),
        gainv=vmem((width // HD, HD), F32),
        hail_sem=pltpu.SemaphoreType.REGULAR((3,)),
        loc_sem=dma((8,)),
        q_sem=dma((2,)),
        kv_send=dma((9, 2)),
        fwd_send=dma((2, 3, 2)),
        kv_recv=dma((9, 2)),
        sib_send=dma((CHIPS,)),
        sib_recv=dma((CHIPS,)),
        w_send=dma((2, 8)),
        w_recv=dma((2, 8)),
        wv_send=dma((16,)),
        wv_recv=dma((16,)),
        a1_send=dma((CHIPS,)),
        a1_recv=dma((CHIPS,)),
        z_send=dma((16,)),
        z_recv=dma((16,)),
        ag_send=dma((2, 2, SIDE)),
        ag_recv=dma((2, SIDE, 2)),
        fin_send=dma((PLANE,)),
        fin_recv=dma((PLANE,)),
    )
    return pl.pallas_call(
        functools.partial(kernel, nt, docs),
        out_shape=jax.ShapeDtypeStruct((orows, width), BF),
        in_specs=[any_spec] * 8,
        out_specs=pl.BlockSpec(memory_space=pltpu.VMEM),
        scratch_shapes=list(scratch.values()),
        compiler_params=pltpu.CompilerParams(
            collective_id=0, has_side_effects=True, vmem_limit_bytes=60 * 1024 * 1024
        ),
        name="attend_project",
    )(
        queries,
        keys,
        values,
        out_weight,
        residual,
        norm_gain.reshape(width // HD, HD),
        lengths,
        owner_blocks.T,
    )


def solution(mesh):
    in_specs = (
        P("ctx", "tp"),
        P("ctx", "tp"),
        P("ctx", "tp"),
        P("tp", None),
        P(("ctx", "tp"), None),
        P(),
        P(),
        P(),
    )
    out_specs = P(("ctx", "tp"), None)
    return jax.shard_map(
        per_device, mesh=mesh, in_specs=in_specs, out_specs=out_specs, check_vma=False
    )
```
